512 devices in a mesh: cells: 128 (over y, z, core), rep: 4 (over x).
Axes of the slice: x: 4, y: 4, z: 16, core: 2. Of those that a mesh axis runs over, the one named last changes fastest.
Arguments:
- particle_speeds: float32 [65536, 3, 128], P(('cells', 'rep')), may hold values from -6 to 6
- particle_diameters: float32 [65536, 128], P(('cells', 'rep')), may hold values from 0.5 to 2
- particle_kelvins: float32 [65536, 128], P(('cells', 'rep')), may hold values from -6 to 6
- unscaled_kernel_coefficients: bfloat16 [65536, 64, 128], P(('cells', 'rep')), may hold values from 0 to 1
- bundle_patch_ordinal: int32 [65536], P(('cells', 'rep')), may hold values from 0 to 255
- bundle_patch_custodian: int32 [65536], P(('cells', 'rep')), may hold values from 0 to 127, as said below
- busy_bundles_per_accelerator: int32 [512], P(('cells', 'rep')), may hold values from 64 to 128, as said below
- ambient_flow_quantities: bfloat16 [32768, 256], P('cells'), may hold values from -24 to 24
Outputs:
- advanced_motion_vector: float32 [65536, 3, 128], P(('cells', 'rep'))
- advanced_thermal_level: float32 [65536, 128], P(('cells', 'rep'))
- forcing_mesh_values: float32 [32768, 256], P(('cells', 'rep'))
The draws below stay inside these ranges and needn't reach their ends.
Inputs may be any that keep to these rules, and one draw needn't show every extreme that they name: `bundle_patch_custodian`: counting all 128 blocks of one device, live or not, no owner is named more than 2 times; one owner, the same on every device, is named exactly 2 times by the live blocks of every device. `busy_bundles_per_accelerator`: some device has all 128 blocks live.
All inputs are finite; a program needn't handle non-finite values.
Results may differ from the reference program's by a relative error of at most 0.00061.
Values may be sent and summed in bfloat16 or wider, within the bound.
A program may use at most 64 MiB of HBM per device.

```python
import math
import jax
import jax.numpy as jnp
from jax import lax

GROUP_POPULATION = 128
PATCH_VOLUMES = 64
GROUPS_ON_CHIPSET = 128
CBO = 256
CAP = 2
SLOTS = 256
GROUP_PLACES_ALL = 65536
VOLUME_PATCHES = 32768


def joint_routes(key):
    base = jax.random.fold_in(key, 101)
    key_count, key_full, key_hot, key_slot, key_block = jax.random.split(base, 5)
    homes = GROUP_PLACES_ALL // GROUPS_ON_CHIPSET
    owners_count = SLOTS // CAP
    lowest = max(CAP, GROUPS_ON_CHIPSET // 2)
    counts_drawn = jax.random.randint(key_count, (homes,), lowest, GROUPS_ON_CHIPSET + 1)
    fullest = jax.random.randint(key_full, (), 0, homes)
    counts_drawn = jnp.where(jnp.arange(homes) == fullest, GROUPS_ON_CHIPSET, counts_drawn).astype(jnp.int32)
    hottest = jax.random.randint(key_hot, (), 0, owners_count)
    slot_ids = jnp.arange(SLOTS, dtype=jnp.int32)
    slot_owner = slot_ids // CAP
    scores = jax.random.randint(key_slot, (homes, SLOTS), 0, 1 << 20) * SLOTS + slot_ids[None, :]
    scores = jnp.where(slot_owner[None, :] == hottest, slot_ids[None, :] - SLOTS, scores)
    sequence = jnp.argsort(scores, axis=1)[:, :GROUPS_ON_CHIPSET] // CAP
    positions = jnp.arange(GROUPS_ON_CHIPSET, dtype=jnp.int32)
    block_scores = jax.random.randint(key_block, (homes, GROUPS_ON_CHIPSET), 0, 1 << 20) * GROUPS_ON_CHIPSET + positions[None, :]
    block_scores = jnp.where(positions[None, :] < counts_drawn[:, None], block_scores, (1 << 30) + positions[None, :])
    ranks = jnp.argsort(jnp.argsort(block_scores, axis=1), axis=1)
    owners = jnp.take_along_axis(sequence, ranks, axis=1)
    return (counts_drawn, owners.reshape(-1).astype(jnp.int32))


def draw_bundle_patch_custodian(key, part):
    return joint_routes(key)[1]


def draw_busy_bundles_per_accelerator(key, part):
    return joint_routes(key)[0]


def set_ends(result, key, low, high):
    longest = result.shape.index(max(result.shape))
    spots = []
    for shift in (0, 1):
        where = [jax.random.randint(jax.random.fold_in(key, axis), (), 0, length) for axis, length in enumerate(result.shape)]
        where[longest] = (where[longest] + shift) % result.shape[longest]
        spots.append(tuple(where))
    return result.at[spots[0]].set(low).at[spots[1]].set(high)


def block_scale(rng, dims, pieces, smallest, high):
    level = 1.0
    for position, blocks in pieces:
        heights = jax.random.uniform(jax.random.fold_in(jax.random.fold_in(rng, 6), position), (blocks,), jnp.float32, smallest / len(pieces), high / len(pieces))
        level = level * jnp.repeat(jnp.exp(heights), dims[position] // blocks).reshape((-1,) + (1,) * (len(dims) - 1 - position))
    return level


def scatter_about(stream_key, dims, scale, most, cuts=(), kind=jnp.bfloat16):
    drawn = scale * jax.random.normal(stream_key, dims, jnp.float32)
    if cuts:
        drawn = drawn * block_scale(stream_key, dims, cuts, -0.22, 0.18)
    return jnp.clip(drawn, -most, most).astype(kind)


def setup_inputs(seed: int = 0) -> dict:
    key_of = jax.random.split(jax.random.key(seed), 9)
    particle_speeds = scatter_about(key_of[0], (GROUP_PLACES_ALL, 3, GROUP_POPULATION), 1.0, 6.0, ((0, 512),), jnp.float32)
    particle_diameters = jnp.clip(jnp.exp(math.log(2.0) - 1.3862944 * jax.random.uniform(key_of[1], (GROUP_PLACES_ALL, GROUP_POPULATION), jnp.float32) ** block_scale(key_of[1], (GROUP_PLACES_ALL, GROUP_POPULATION), ((0, 512),), -0.2, 0.2)), 0.5, 2.0)
    particle_kelvins = scatter_about(key_of[2], (GROUP_PLACES_ALL, GROUP_POPULATION), 1.0, 6.0, ((0, 512),), jnp.float32)
    unscaled_kernel_coefficients = jnp.clip(1.0 * jax.random.uniform(key_of[3], (GROUP_PLACES_ALL, PATCH_VOLUMES, GROUP_POPULATION), jnp.float32) ** block_scale(key_of[3], (GROUP_PLACES_ALL, PATCH_VOLUMES, GROUP_POPULATION), ((0, 512),), -0.2, 0.2), 0.0, 1.0).astype(jnp.bfloat16)
    bundle_patch_ordinal = set_ends(jax.random.randint(key_of[4], (GROUP_PLACES_ALL,), 0, CBO), jax.random.fold_in(key_of[4], 1), 0, CBO - 1).astype(jnp.int32)
    bundle_patch_custodian = draw_bundle_patch_custodian(jax.random.fold_in(key_of[8], 71), 0)
    busy_bundles_per_accelerator = draw_busy_bundles_per_accelerator(jax.random.fold_in(key_of[8], 71), 0)
    ambient_flow_quantities = scatter_about(key_of[7], (VOLUME_PATCHES, 4 * PATCH_VOLUMES), 4.0, 24.0, ((0, 128),))
    return {"particle_speeds": particle_speeds, "particle_diameters": particle_diameters, "particle_kelvins": particle_kelvins, "unscaled_kernel_coefficients": unscaled_kernel_coefficients, "bundle_patch_ordinal": bundle_patch_ordinal, "bundle_patch_custodian": bundle_patch_custodian, "busy_bundles_per_accelerator": busy_bundles_per_accelerator, "ambient_flow_quantities": ambient_flow_quantities}


REYNOLDS_SCALE = 20.0
DRAG_SCALE = 1.0
HEAT_SCALE = 0.5
PRANDTL_ROOT = 0.9
LOADING = 0.2

def integrate_timestep(looked_up, tiles_here, parcel_velocity, parcel_diameter, parcel_heat):
    blocks_here = looked_up.shape[0]
    cells_block = tiles_here.shape[1]
    scale = 2.0 / cells_block
    cell_values = looked_up.reshape(blocks_here, 4, cells_block).astype(jnp.float32)
    tiles_wide = tiles_here.astype(jnp.float32)
    sampled = jnp.einsum('nck,nkp->ncp', cell_values, tiles_wide, precision=lax.Precision.HIGHEST) * scale
    gas_velocity = sampled[:, :3]
    warmth = sampled[:, 3]
    slip_velocity = gas_velocity - parcel_velocity
    slip_speed = jnp.sqrt(1.0 + lax.optimization_barrier(jnp.sum(slip_velocity * slip_velocity, axis=1)))
    reynolds = REYNOLDS_SCALE * parcel_diameter * slip_speed
    squared = parcel_diameter * parcel_diameter
    drag_rate = DRAG_SCALE * (1.0 + 0.15 * reynolds ** 0.687) / squared
    heat_rate = HEAT_SCALE * (2.0 + 0.6 * PRANDTL_ROOT * jnp.sqrt(reynolds)) / squared
    relocated_bundles = (parcel_velocity + drag_rate[:, None] * gas_velocity) / (1.0 + drag_rate[:, None])
    particles_after_heating = (parcel_heat + heat_rate * warmth) / (1.0 + heat_rate)
    parcel_mass = LOADING * parcel_diameter * squared
    momentum_heat = jnp.concatenate([-parcel_mass[:, None] * (relocated_bundles - parcel_velocity), (-parcel_mass * (particles_after_heating - parcel_heat))[:, None]], axis=1)
    rounded = lax.optimization_barrier(momentum_heat.astype(jnp.bfloat16))
    coupling_terms = jnp.einsum('ncp,nkp->nck', rounded.astype(jnp.float32), tiles_wide, precision=lax.Precision.HIGHEST) * scale
    return (relocated_bundles, particles_after_heating, coupling_terms.reshape(blocks_here, 4 * cells_block))

def reference(particle_speeds, particle_diameters, particle_kelvins, unscaled_kernel_coefficients, bundle_patch_ordinal, bundle_patch_custodian, busy_bundles_per_accelerator, ambient_flow_quantities):
    homes = GROUP_PLACES_ALL // GROUPS_ON_CHIPSET

    def advance_home(accumulator, home_index):
        front_entry = (home_index * GROUPS_ON_CHIPSET).astype(jnp.int32)
        native_particle_speed = lax.dynamic_slice_in_dim(particle_speeds, front_entry, GROUPS_ON_CHIPSET, 0)
        native_particle_size = lax.dynamic_slice_in_dim(particle_diameters, front_entry, GROUPS_ON_CHIPSET, 0)
        custodian_enthalpy_gain = lax.dynamic_slice_in_dim(particle_kelvins, front_entry, GROUPS_ON_CHIPSET, 0)
        native_bundle_arrays = lax.dynamic_slice_in_dim(unscaled_kernel_coefficients, front_entry, GROUPS_ON_CHIPSET, 0)
        home_cells = lax.dynamic_slice_in_dim(bundle_patch_ordinal, front_entry, GROUPS_ON_CHIPSET, 0)
        home_owner = lax.dynamic_slice_in_dim(bundle_patch_custodian, front_entry, GROUPS_ON_CHIPSET, 0)
        lookup_lines = (home_owner * CBO + home_cells).astype(jnp.int32)
        relocated_bundles, particles_after_heating, coupling_terms = integrate_timestep(ambient_flow_quantities[lookup_lines], native_bundle_arrays, native_particle_speed, native_particle_size, custodian_enthalpy_gain)
        active_groups = jnp.arange(GROUPS_ON_CHIPSET, dtype=jnp.int32) < busy_bundles_per_accelerator[home_index]
        relocated_bundles = jnp.where(active_groups[:, None, None], relocated_bundles, native_particle_speed)
        particles_after_heating = jnp.where(active_groups[:, None], particles_after_heating, custodian_enthalpy_gain)
        coupling_terms = jnp.where(active_groups[:, None], coupling_terms, jnp.zeros_like(coupling_terms))
        accumulator = accumulator.at[lookup_lines].add(coupling_terms)
        return (accumulator, (relocated_bundles, particles_after_heating))
    start_field = jnp.zeros((VOLUME_PATCHES, 4 * PATCH_VOLUMES), jnp.float32)
    forcing_mesh_values, (moved_all, warmed_all) = lax.scan(advance_home, start_field, jnp.arange(homes, dtype=jnp.int32))
    return (moved_all.reshape(GROUP_PLACES_ALL, 3, GROUP_POPULATION), warmed_all.reshape(GROUP_PLACES_ALL, GROUP_POPULATION), forcing_mesh_values)
```

```python
import functools

import jax
import jax.numpy as jnp
from jax import lax
from jax.experimental import pallas as pl
from jax.experimental.pallas import tpu as pltpu
from jax.sharding import PartitionSpec as P

MESH = pl.DeviceIdType.MESH
F32, BF16, I32 = jnp.float32, jnp.bfloat16, jnp.int32

REYNOLDS_SCALE = 20.0
DRAG_SCALE = 1.0
HEAT_SCALE = 0.5
PRANDTL_ROOT = 0.9
LOADING = 0.2
ABSENT = 1.0e9


def iota(shape, axis):
    return lax.broadcasted_iota(I32, shape, axis)


def to_row(column):
    n = column.shape[0]
    eye = iota((n, n), 0) == iota((n, n), 1)
    return jnp.sum(jnp.where(eye, column, 0.0), axis=0, keepdims=True)


def to_column(row):
    n = row.shape[1]
    eye = iota((n, n), 0) == iota((n, n), 1)
    return jnp.sum(jnp.where(eye, row, 0.0), axis=1, keepdims=True)


def halves(x):
    high = x.astype(BF16)
    return high, (x - high.astype(F32)).astype(BF16)


def dot(a, b):
    return jnp.dot(a, b, preferred_element_type=F32)


def step_kernel(
    nz,
    ncore,
    na,
    nrep,
    owner_ref,
    place_ref,
    busy_ref,
    field_ref,
    tiles_hbm,
    speed_hbm,
    size_hbm,
    heat_hbm,
    moved_hbm,
    warmed_hbm,
    source_ref,
    tiles,
    speed,
    size,
    heat,
    moved,
    warmed,
    lab_a,
    lab_z,
    row_zs,
    row_zr,
    row_as,
    row_ar,
    sums_as,
    sums_ar,
    sums_zs,
    sums_zr,
    part_s,
    part_r,
    in_sem,
    out_sem,
    send_sem,
    recv_sem,
):
    blocks = tiles.shape[0]
    cells = tiles.shape[1]
    width = 4 * cells
    owned = field_ref.shape[0]
    sources = nz * na
    slots = 2 * sources
    me = lax.axis_index("cells")
    r = lax.axis_index("rep")
    core = lax.rem(me, ncore)
    z = lax.rem(me // ncore, nz)
    y = me // (ncore * nz)
    a = y * ncore + core

    def at_z(step):
        other = lax.rem(z + step, nz)
        return other, {"cells": (y * nz + other) * ncore + core, "rep": r}

    def at_a(step):
        other = lax.rem(a + step, na)
        return other, {
            "cells": ((other // ncore) * nz + z) * ncore + lax.rem(other, ncore),
            "rep": r,
        }

    def at_r(step):
        other = lax.rem(r + step, nrep)
        return other, {"cells": me, "rep": other}

    inputs = [
        pltpu.make_async_copy(src, dst, in_sem.at[i])
        for i, (src, dst) in enumerate(
            ((tiles_hbm, tiles), (speed_hbm, speed), (size_hbm, size), (heat_hbm, heat))
        )
    ]
    for copy in inputs:
        copy.start()

    barrier = pltpu.get_barrier_semaphore()
    for where, count in ((at_z, nz), (at_a, na), (at_r, nrep)):
        for step in range(1, count):
            pl.semaphore_signal(
                barrier, inc=1, device_id=where(step)[1], device_id_type=MESH
            )
    pl.semaphore_wait(barrier, nz + na + nrep - 3)

    def exchange(phase, where, count, source, target, mine):
        for step in range(1, count):
            other, device = where(step)
            pltpu.make_async_remote_copy(
                src_ref=source(other),
                dst_ref=target.at[mine],
                send_sem=send_sem.at[phase],
                recv_sem=recv_sem.at[phase],
                device_id=device,
                device_id_type=MESH,
            ).start()

    def arrived(phase, where, count, target):
        some = target.at[pl.ds(0, count - 1)]
        pltpu.make_async_remote_copy(
            src_ref=some,
            dst_ref=some,
            send_sem=send_sem.at[phase],
            recv_sem=recv_sem.at[phase],
            device_id=where(1)[1],
            device_id_type=MESH,
        ).wait()

    owner = owner_ref[...]
    live = iota((1, blocks), 1) < busy_ref[0]
    label = jnp.where(live, owner * owned + place_ref[...], -1)
    lab_a[a] = label
    exchange(0, at_a, na, lambda other: lab_a.at[a], lab_a, a)

    ownerf = owner.astype(F32)
    earlier = (
        (to_column(ownerf) == ownerf)
        & (iota((blocks, blocks), 0) < iota((blocks, blocks), 1))
        & (iota((blocks, blocks), 0) < busy_ref[0])
    )
    rank = jnp.sum(jnp.where(earlier, 1.0, 0.0), axis=0, keepdims=True).astype(I32)
    owner_y = owner // (nz * ncore)
    owner_rest = owner - owner_y * (nz * ncore)
    owner_z = owner_rest // ncore
    owner_a = owner_y * ncore + (owner_rest - owner_z * ncore)
    slot = jnp.where(live, owner_a * (2 * nz) + rank * nz + owner_z, -1)
    slot_column = to_column(slot.astype(F32))
    to_slots = jnp.where(iota((slots, blocks), 0) == slot, 1.0, 0.0).astype(BF16)
    from_slots = jnp.where(
        iota((blocks, slots), 1).astype(F32) == slot_column, 1.0, 0.0
    ).astype(BF16)

    arrived(0, at_a, na, lab_a)
    lab_z[z] = lab_a[...].reshape(na, blocks)
    exchange(1, at_z, nz, lambda other: lab_z.at[z], lab_z, z)
    arrived(1, at_z, nz, lab_z)

    place = lab_z[...].reshape(sources, blocks) - me * owned
    match = (place >= 0) & (place < owned)
    key = (iota((sources, blocks), 1) * owned + place).astype(F32)
    first = jnp.min(jnp.where(match, key, ABSENT), axis=1, keepdims=True)
    last = jnp.max(jnp.where(match, key, -1.0), axis=1, keepdims=True)
    size_f = float(owned)
    place_0 = jnp.where(first < ABSENT, first - jnp.floor(first / size_f) * size_f, -1.0)
    place_1 = jnp.where(last > first, last - jnp.floor(last / size_f) * size_f, -1.0)
    lanes = iota((sources, owned), 1).astype(F32)
    field = field_ref[...]
    rows = [
        dot(jnp.where(lanes == p, 1.0, 0.0).astype(BF16), field).reshape(nz, na, width)
        for p in (place_0, place_1)
    ]
    row_zs[...] = jnp.concatenate(rows, axis=1).astype(BF16)
    exchange(2, at_z, nz, lambda other: row_zs.at[other], row_zr, z)
    row_zr[z] = row_zs[z]
    deposits = [
        jnp.where(
            iota((owned, sources), 0).astype(F32) == to_row(p), 1.0, 0.0
        ).astype(BF16)
        for p in (place_0, place_1)
    ]

    out_row, in_row = iota((slots, slots), 0), iota((slots, slots), 1)
    out_a = out_row // (2 * nz)
    out_rest = out_row - out_a * (2 * nz)
    out_rank = out_rest // nz
    out_z = out_rest - out_rank * nz
    regroup = jnp.where(
        in_row == out_z * (2 * na) + out_rank * na + out_a, 1.0, 0.0
    ).astype(BF16)
    arrived(2, at_z, nz, row_zr)
    row_as[...] = (
        dot(regroup, row_zr[...].reshape(slots, width))
        .astype(BF16)
        .reshape(na, 2 * nz, width)
    )
    exchange(3, at_a, na, lambda other: row_as.at[other], row_ar, a)
    row_ar[a] = row_as[a]
    spread_in, spread_out = iota((width, 8 * cells), 0), iota((width, 8 * cells), 1)
    out_c = spread_out // (2 * cells)
    out_k = spread_out - (spread_out // cells) * cells
    spread = jnp.where(spread_in == out_c * cells + out_k, 1.0, 0.0).astype(BF16)
    arrived(3, at_a, na, row_ar)

    gas = dot(from_slots, row_ar[...].reshape(slots, width)).astype(BF16)
    gas = dot(gas, spread)
    for copy in inputs:
        copy.wait()
    diagonal = iota((8, 8 * cells), 1) // cells == iota((8, 8 * cells), 0)
    pair = 2 * cells
    sampled = []
    for g in range(blocks // 8):
        left = []
        for c in range(4):
            piece = gas[8 * g : 8 * g + 8, c * pair : (c + 1) * pair]
            left.append(
                jnp.where(diagonal, jnp.concatenate([piece] * 4, axis=1), 0.0)
            )
        left = jnp.concatenate(left, axis=0).astype(BF16)
        sampled.append(
            dot(left, tiles[8 * g : 8 * g + 8].reshape(8 * cells, tiles.shape[2]))
        )
    scale = 2.0 / cells
    u = [
        jnp.concatenate([s[8 * c : 8 * c + 8] for s in sampled], axis=0) * scale
        for c in range(4)
    ]

    v = [speed[c] for c in range(3)]
    d = size[...]
    t = heat[...]
    slip = [u[c] - v[c] for c in range(3)]
    slip_speed = jnp.sqrt(
        1.0 + (slip[0] * slip[0] + slip[1] * slip[1] + slip[2] * slip[2])
    )
    reynolds = REYNOLDS_SCALE * d * slip_speed
    squared = d * d
    drag = DRAG_SCALE * (1.0 + 0.15 * jnp.exp(0.687 * jnp.log(reynolds))) / squared
    warm = HEAT_SCALE * (2.0 + 0.6 * PRANDTL_ROOT * jnp.sqrt(reynolds)) / squared
    mass = LOADING * d * squared
    live_column = slot_column >= 0.0
    terms = []
    for c in range(3):
        new = (v[c] + drag * u[c]) / (1.0 + drag)
        terms.append((-mass * (new - v[c])).astype(BF16))
        moved[c] = jnp.where(live_column, new, v[c])
    new = (t + warm * u[3]) / (1.0 + warm)
    terms.append((-mass * (new - t)).astype(BF16))
    warmed[...] = jnp.where(live_column, new, t)
    outputs = [
        pltpu.make_async_copy(src, dst, out_sem.at[i])
        for i, (src, dst) in enumerate(((moved, moved_hbm), (warmed, warmed_hbm)))
    ]
    for copy in outputs:
        copy.start()

    lane, line = iota((32, pair), 1), iota((32, pair), 0)
    line = line - (line // 8) * 8
    low = iota((8, pair), 1) < cells
    rows = []
    termf = [x.astype(F32) for x in terms]
    for g in range(blocks // 8):
        left = jnp.concatenate([x[8 * g : 8 * g + 8] for x in termf], axis=0)
        full = lax.dot_general(
            left.astype(BF16),
            tiles[8 * g : 8 * g + 8].reshape(8 * cells, tiles.shape[2]),
            (((1,), (1,)), ((), ())),
            preferred_element_type=F32,
        )
        own = jnp.zeros((32, pair), F32)
        for j in range(4):
            keep = line == 2 * j + lane // cells
            own = own + jnp.where(keep, full[:, j * pair : (j + 1) * pair], 0.0)
        own = own + pltpu.roll(own, cells, axis=1)
        rows.append(
            jnp.concatenate(
                [
                    jnp.where(low, own[0:8], own[8:16]),
                    jnp.where(low, own[16:24], own[24:32]),
                ],
                axis=1,
            )
        )
    high, rest = halves(jnp.concatenate(rows, axis=0) * scale)
    slotted = (dot(to_slots, high) + dot(to_slots, rest)).reshape(na, 2 * nz, width)
    group = 4 * nz
    sums_as[...] = jnp.concatenate(
        [slotted[..., :128], slotted[..., 128:]], axis=1
    ).reshape(na * group, 128)

    def of_group(ref, other):
        return ref.at[pl.ds(pl.multiple_of(other * group, group), group)]

    for step in range(1, na):
        other, device = at_a(step)
        pltpu.make_async_remote_copy(
            src_ref=of_group(sums_as, other),
            dst_ref=of_group(sums_ar, a),
            send_sem=send_sem.at[4],
            recv_sem=recv_sem.at[4],
            device_id=device,
            device_id_type=MESH,
        ).start()
    mine = pl.ds(pl.multiple_of(a * group, group), group)
    sums_ar[mine, :] = sums_as[mine, :]
    some = sums_ar.at[pl.ds(0, (na - 1) * group)]
    pltpu.make_async_remote_copy(
        src_ref=some,
        dst_ref=some,
        send_sem=send_sem.at[4],
        recv_sem=recv_sem.at[4],
        device_id=at_a(1)[1],
        device_id_type=MESH,
    ).wait()
    for other in range(nz):
        for k in range(2):
            for half in range(2):
                sums_zs[other, pl.ds(k * na, na), pl.ds(128 * half, 128)] = sums_ar[
                    pl.ds((2 * half + k) * nz + other, na, stride=group), :
                ]
    exchange(5, at_z, nz, lambda other: sums_zs.at[other], sums_zr, z)
    sums_zr[z] = sums_zs[z]
    arrived(5, at_z, nz, sums_zr)

    total = jnp.zeros((owned, width), F32)
    for k in range(2):
        got = sums_zr[:, k * na : (k + 1) * na, :].reshape(sources, width)
        high, rest = halves(got)
        total = total + dot(deposits[k], high) + dot(deposits[k], rest)
    part_s[...] = total.reshape(nrep, owned // nrep, width)
    exchange(6, at_r, nrep, lambda other: part_s.at[other], part_r, r)
    part_r[r] = part_s[r]
    arrived(6, at_r, nrep, part_r)
    total = part_r[0]
    for k in range(1, nrep):
        total = total + part_r[k]
    source_ref[...] = total
    for copy in outputs:
        copy.wait()


def per_device(
    ny,
    nz,
    ncore,
    nrep,
    particle_speeds,
    particle_diameters,
    particle_kelvins,
    unscaled_kernel_coefficients,
    bundle_patch_ordinal,
    bundle_patch_custodian,
    busy_bundles_per_accelerator,
    ambient_flow_quantities,
):
    blocks, cells, parcels = unscaled_kernel_coefficients.shape
    owned, width = ambient_flow_quantities.shape
    na = ny * ncore
    sources = na * nz
    slots = 2 * sources
    anywhere = pl.BlockSpec(memory_space=pl.ANY)
    vmem = pl.BlockSpec(memory_space=pltpu.VMEM)
    smem = pl.BlockSpec(memory_space=pltpu.SMEM)
    moved, warmed, source = pl.pallas_call(
        functools.partial(step_kernel, nz, ncore, na, nrep),
        out_shape=(
            jax.ShapeDtypeStruct((3, blocks, parcels), F32),
            jax.ShapeDtypeStruct((blocks, parcels), F32),
            jax.ShapeDtypeStruct((owned // nrep, width), F32),
        ),
        in_specs=[vmem, vmem, smem, vmem] + [anywhere] * 4,
        out_specs=(anywhere, anywhere, vmem),
        scratch_shapes=[
            pltpu.VMEM((blocks, cells, parcels), BF16),
            pltpu.VMEM((3, blocks, parcels), F32),
            pltpu.VMEM((blocks, parcels), F32),
            pltpu.VMEM((blocks, parcels), F32),
            pltpu.VMEM((3, blocks, parcels), F32),
            pltpu.VMEM((blocks, parcels), F32),
            pltpu.VMEM((na, 1, blocks), I32),
            pltpu.VMEM((nz, na, blocks), I32),
            pltpu.VMEM((nz, 2 * na, width), BF16),
            pltpu.VMEM((nz, 2 * na, width), BF16),
            pltpu.VMEM((na, 2 * nz, width), BF16),
            pltpu.VMEM((na, 2 * nz, width), BF16),
            pltpu.VMEM((2 * slots, width // 2), F32),
            pltpu.VMEM((2 * slots, width // 2), F32),
            pltpu.VMEM((nz, 2 * na, width), F32),
            pltpu.VMEM((nz, 2 * na, width), F32),
            pltpu.VMEM((nrep, owned // nrep, width), F32),
            pltpu.VMEM((nrep, owned // nrep, width), F32),
            pltpu.SemaphoreType.DMA((4,)),
            pltpu.SemaphoreType.DMA((2,)),
            pltpu.SemaphoreType.DMA((7,)),
            pltpu.SemaphoreType.DMA((7,)),
        ],
        compiler_params=pltpu.CompilerParams(
            collective_id=0, has_side_effects=True, vmem_limit_bytes=40 * 2**20
        ),
        name="parcel_step",
    )(
        bundle_patch_custodian.reshape(1, blocks),
        bundle_patch_ordinal.reshape(1, blocks),
        busy_bundles_per_accelerator,
        ambient_flow_quantities,
        unscaled_kernel_coefficients,
        jnp.transpose(particle_speeds, (1, 0, 2)),
        particle_diameters,
        particle_kelvins,
    )
    return jnp.transpose(moved, (1, 0, 2)), warmed, source


def solution(mesh, ny=4, nz=16, ncore=2):
    both = ("cells", "rep")
    return jax.shard_map(
        functools.partial(per_device, ny, nz, ncore, mesh.shape["rep"]),
        mesh=mesh,
        in_specs=(
            P(both, None, None),
            P(both, None),
            P(both, None),
            P(both, None, None),
            P(both),
            P(both),
            P(both),
            P("cells", None),
        ),
        out_specs=(P(both, None, None), P(both, None), P(both, None)),
        check_vma=False,
    )
```

```python
import functools

import jax
import jax.numpy as jnp
from jax import lax
from jax.experimental import pallas as pl
from jax.experimental.pallas import tpu as pltpu
from jax.sharding import PartitionSpec as P

MESH = pl.DeviceIdType.MESH
F32, BF16, I32 = jnp.float32, jnp.bfloat16, jnp.int32

REYNOLDS_SCALE = 20.0
DRAG_SCALE = 1.0
HEAT_SCALE = 0.5
PRANDTL_ROOT = 0.9
LOADING = 0.2
ABSENT = 1.0e9


def iota(shape, axis):
    return lax.broadcasted_iota(I32, shape, axis)


def to_row(column):
    n = column.shape[0]
    eye = iota((n, n), 0) == iota((n, n), 1)
    return jnp.sum(jnp.where(eye, column, 0.0), axis=0, keepdims=True)


def to_column(row):
    n = row.shape[1]
    eye = iota((n, n), 0) == iota((n, n), 1)
    return jnp.sum(jnp.where(eye, row, 0.0), axis=1, keepdims=True)


def halves(x):
    high = x.astype(BF16)
    return high, (x - high.astype(F32)).astype(BF16)


def dot(a, b):
    return jnp.dot(a, b, preferred_element_type=F32)


def step_kernel(
    ny,
    nz,
    nrep,
    owner_hbm,
    place_hbm,
    busy_ref,
    field_hbm,
    tiles_hbm,
    speed_hbm,
    size_hbm,
    heat_hbm,
    moved_hbm,
    warmed_hbm,
    source_ref,
    owner_v,
    place_v,
    field_v,
    tiles,
    speed,
    size,
    heat,
    moved,
    warmed,
    lab_mine,
    lab_other,
    lab_all,
    row_s,
    row_r,
    row_x,
    sums_x,
    sums_s,
    sums_r,
    part_s,
    part_r,
    in_sem,
    out_sem,
    send_sem,
    recv_sem,
):
    blocks, cells, parcels = tiles.shape
    width = 4 * cells
    owned = field_v.shape[0]
    chips = ny * nz
    sources = 2 * chips
    slots = 2 * sources
    me = lax.axis_index("cells")
    r = lax.axis_index("rep")
    core = me & 1
    chip = me >> 1
    z = chip & (nz - 1)
    y = chip // nz
    steps = sorted(
        ((dy, dz) for dy in range(ny) for dz in range(nz) if dy or dz),
        key=lambda step: (
            -min(step[0], ny - step[0]) - min(step[1], nz - step[1]),
            step,
        ),
    )
    others = []
    for dy, dz in steps:
        other = ((y + dy) & (ny - 1)) * nz + ((z + dz) & (nz - 1))
        others.append((other, {"cells": other * 2 + core, "rep": r}))
    sibling = {"cells": chip * 2 + (1 - core), "rep": r}
    reps = []
    for step in range(1, nrep):
        other = (r + step) & (nrep - 1)
        reps.append((other, {"cells": me, "rep": other}))

    inputs = [
        pltpu.make_async_copy(src, dst, in_sem.at[i])
        for i, (src, dst) in enumerate(
            (
                (owner_hbm, owner_v),
                (place_hbm, place_v),
                (field_hbm, field_v),
                (tiles_hbm, tiles),
                (speed_hbm, speed),
                (size_hbm, size),
                (heat_hbm, heat),
            )
        )
    ]
    for copy in inputs:
        copy.start()

    barrier = pltpu.get_barrier_semaphore()
    for device in [device for _, device in others + reps] + [sibling]:
        pl.semaphore_signal(barrier, inc=1, device_id=device, device_id_type=MESH)

    def send(phase, src, dst, device):
        copy = pltpu.make_async_remote_copy(
            src_ref=src,
            dst_ref=dst,
            send_sem=send_sem.at[phase],
            recv_sem=recv_sem.at[phase],
            device_id=device,
            device_id_type=MESH,
        )
        copy.start()
        return copy

    def arrived(phase, some):
        pltpu.make_async_remote_copy(
            src_ref=some,
            dst_ref=some,
            send_sem=send_sem.at[phase],
            recv_sem=recv_sem.at[phase],
            device_id=sibling,
            device_id_type=MESH,
        ).wait()

    target = iota((1, 8 * cells), 1)
    target = (target // (2 * cells)) * cells + (target & (cells - 1))
    spread = jnp.where(iota((width, 8 * cells), 0) == target, 1.0, 0.0).astype(BF16)
    diagonal = (iota((1, 8 * cells), 1) // cells) == iota((8, 1), 0)
    slot_line = iota((slots, 1), 0)
    slot_rank = slot_line & 1
    slot_source = ((slot_line & (sources - 1)) >> 1) * 2 + slot_line // sources

    inputs[0].wait()
    inputs[1].wait()
    owner = owner_v[...]
    live = iota((1, blocks), 1) < busy_ref[0]
    label = jnp.where(live, owner * owned + place_v[...], -1)
    lab_mine[...] = label

    ownerf = owner.astype(F32)
    earlier = (
        (to_column(ownerf) == ownerf)
        & (iota((blocks, blocks), 0) < iota((blocks, blocks), 1))
        & (iota((blocks, blocks), 0) < busy_ref[0])
    )
    rank = jnp.sum(jnp.where(earlier, 1.0, 0.0), axis=0, keepdims=True).astype(I32)
    slot = jnp.where((owner & 1) == core, 0, sources) + (owner >> 1) * 2 + rank
    slot = jnp.where(live, slot, -1)
    slot_column = to_column(slot.astype(F32))
    to_slots = jnp.where(slot_line == slot, 1.0, 0.0).astype(BF16)
    from_slots = jnp.where(
        iota((1, slots), 1).astype(F32) == slot_column, 1.0, 0.0
    ).astype(BF16)

    pl.semaphore_wait(barrier, chips - 1 + nrep - 1 + 1)

    send(0, lab_mine, lab_other, sibling).wait()
    got = lab_other[...]
    lab_all[chip] = jnp.concatenate(
        [jnp.where(core == 0, label, got), jnp.where(core == 0, got, label)], axis=0
    )
    for other, device in others:
        send(1, lab_all.at[chip], lab_all.at[chip], device)
    arrived(1, lab_all.at[pl.ds(0, chips - 1)])

    place = lab_all[...].reshape(sources, blocks) - me * owned
    match = (place >= 0) & (place < owned)
    key = (iota((sources, blocks), 1) * owned + place).astype(F32)
    first = jnp.min(jnp.where(match, key, ABSENT), axis=1, keepdims=True)
    last = jnp.max(jnp.where(match, key, -1.0), axis=1, keepdims=True)
    size_f = float(owned)
    place_0 = jnp.where(first < ABSENT, first - jnp.floor(first / size_f) * size_f, -1.0)
    place_1 = jnp.where(last > first, last - jnp.floor(last / size_f) * size_f, -1.0)
    wanted = jnp.sum(
        jnp.where(
            iota((1, sources), 1) == slot_source,
            jnp.where(slot_rank == 0, to_row(place_0), to_row(place_1)),
            0.0,
        ),
        axis=1,
        keepdims=True,
    )
    picks = jnp.where(iota((1, owned), 1).astype(F32) == wanted, 1.0, 0.0).astype(BF16)
    inputs[2].wait()
    row_s[...] = dot(picks, field_v[...]).astype(BF16).reshape(2, chips, 2, width)
    for other, device in others:
        send(2, row_s.at[:, other], row_r.at[:, chip], device)
    row_r[:, chip] = row_s[:, chip]
    lane = iota((1, slots), 1)
    given = jnp.sum(
        jnp.where(
            iota((sources, 1), 0) == (lane >> 1),
            jnp.where((lane & 1) == 0, place_0, place_1),
            0.0,
        ),
        axis=0,
        keepdims=True,
    )
    deposits = jnp.where(iota((owned, 1), 0).astype(F32) == given, 1.0, 0.0).astype(BF16)
    arrived(2, row_r.at[:, pl.ds(0, chips - 1)])
    copy = send(3, row_r.at[1 - core], row_x, sibling)
    gas = dot(from_slots[:, :sources], row_r[core].reshape(sources, width))
    copy.wait()

    gas = gas + dot(from_slots[:, sources:], row_x[...].reshape(sources, width))
    gas = dot(gas.astype(BF16), spread)
    for copy in inputs[3:]:
        copy.wait()
    pair = 2 * cells
    sampled = []
    for g in range(blocks // 8):
        left = []
        for c in range(4):
            piece = gas[8 * g : 8 * g + 8, c * pair : (c + 1) * pair]
            left.append(
                jnp.where(diagonal, jnp.concatenate([piece] * 4, axis=1), 0.0)
            )
        left = jnp.concatenate(left, axis=0).astype(BF16)
        sampled.append(
            dot(left, tiles[8 * g : 8 * g + 8].reshape(8 * cells, parcels))
        )
    scale = 2.0 / cells
    u = [
        jnp.concatenate([s[8 * c : 8 * c + 8] for s in sampled], axis=0) * scale
        for c in range(4)
    ]

    v = [speed[c] for c in range(3)]
    d = size[...]
    t = heat[...]
    slip = [u[c] - v[c] for c in range(3)]
    slip_speed = jnp.sqrt(
        1.0 + (slip[0] * slip[0] + slip[1] * slip[1] + slip[2] * slip[2])
    )
    reynolds = REYNOLDS_SCALE * d * slip_speed
    squared = d * d
    drag = DRAG_SCALE * (1.0 + 0.15 * jnp.exp(0.687 * jnp.log(reynolds))) / squared
    warm = HEAT_SCALE * (2.0 + 0.6 * PRANDTL_ROOT * jnp.sqrt(reynolds)) / squared
    mass = LOADING * d * squared
    live_column = slot_column >= 0.0
    terms = []
    for c in range(3):
        new = (v[c] + drag * u[c]) / (1.0 + drag)
        terms.append((-mass * (new - v[c])).astype(BF16))
        moved[c] = jnp.where(live_column, new, v[c])
    new = (t + warm * u[3]) / (1.0 + warm)
    terms.append((-mass * (new - t)).astype(BF16))
    warmed[...] = jnp.where(live_column, new, t)
    outputs = [
        pltpu.make_async_copy(src, dst, out_sem.at[i])
        for i, (src, dst) in enumerate(((moved, moved_hbm), (warmed, warmed_hbm)))
    ]
    for copy in outputs:
        copy.start()

    lane, line = iota((32, pair), 1), iota((32, pair), 0)
    line = line & 7
    low = iota((8, pair), 1) < cells
    rows = []
    termf = [x.astype(F32) for x in terms]
    for g in range(blocks // 8):
        left = jnp.concatenate([x[8 * g : 8 * g + 8] for x in termf], axis=0)
        full = lax.dot_general(
            left.astype(BF16),
            tiles[8 * g : 8 * g + 8].reshape(8 * cells, parcels),
            (((1,), (1,)), ((), ())),
            preferred_element_type=F32,
        )
        own = jnp.zeros((32, pair), F32)
        for j in range(4):
            keep = line == 2 * j + lane // cells
            own = own + jnp.where(keep, full[:, j * pair : (j + 1) * pair], 0.0)
        own = own + pltpu.roll(own, cells, axis=1)
        rows.append(
            jnp.concatenate(
                [
                    jnp.where(low, own[0:8], own[8:16]),
                    jnp.where(low, own[16:24], own[24:32]),
                ],
                axis=1,
            )
        )
    high, rest = halves(jnp.concatenate(rows, axis=0) * scale)

    leave = to_slots[sources:]
    sums_x[...] = (dot(leave, high) + dot(leave, rest)).reshape(chips, 2, width)
    copy = send(4, sums_x, sums_s.at[:, core], sibling)
    stay = to_slots[:sources]
    sums_s[:, core] = (dot(stay, high) + dot(stay, rest)).reshape(chips, 2, width)
    copy.wait()
    for other, device in others:
        send(5, sums_s.at[other], sums_r.at[chip], device)
    sums_r[chip] = sums_s[chip]
    arrived(5, sums_r.at[pl.ds(0, chips - 1)])

    high, rest = halves(sums_r[...].reshape(slots, width))
    total = dot(deposits, high) + dot(deposits, rest)
    part_s[...] = total.reshape(nrep, owned // nrep, width)
    for other, device in reps:
        send(6, part_s.at[other], part_r.at[r], device)
    part_r[r] = part_s[r]
    arrived(6, part_r.at[pl.ds(0, nrep - 1)])
    total = part_r[0]
    for k in range(1, nrep):
        total = total + part_r[k]
    source_ref[...] = total
    for copy in outputs:
        copy.wait()


def per_device(
    ny,
    nz,
    nrep,
    particle_speeds,
    particle_diameters,
    particle_kelvins,
    unscaled_kernel_coefficients,
    bundle_patch_ordinal,
    bundle_patch_custodian,
    busy_bundles_per_accelerator,
    ambient_flow_quantities,
):
    blocks, cells, parcels = unscaled_kernel_coefficients.shape
    owned, width = ambient_flow_quantities.shape
    chips = ny * nz
    hbm = pl.BlockSpec(memory_space=pltpu.HBM)
    vmem = pl.BlockSpec(memory_space=pltpu.VMEM)
    smem = pl.BlockSpec(memory_space=pltpu.SMEM)
    moved, warmed, source = pl.pallas_call(
        functools.partial(step_kernel, ny, nz, nrep),
        out_shape=(
            jax.ShapeDtypeStruct((3, blocks, parcels), F32),
            jax.ShapeDtypeStruct((blocks, parcels), F32),
            jax.ShapeDtypeStruct((owned // nrep, width), F32),
        ),
        in_specs=[hbm, hbm, smem] + [hbm] * 5,
        out_specs=(hbm, hbm, vmem),
        scratch_shapes=[
            pltpu.VMEM((1, blocks), I32),
            pltpu.VMEM((1, blocks), I32),
            pltpu.VMEM((owned, width), BF16),
            pltpu.VMEM((blocks, cells, parcels), BF16),
            pltpu.VMEM((3, blocks, parcels), F32),
            pltpu.VMEM((blocks, parcels), F32),
            pltpu.VMEM((blocks, parcels), F32),
            pltpu.VMEM((3, blocks, parcels), F32),
            pltpu.VMEM((blocks, parcels), F32),
            pltpu.VMEM((1, blocks), I32),
            pltpu.VMEM((1, blocks), I32),
            pltpu.VMEM((chips, 2, blocks), I32),
            pltpu.VMEM((2, chips, 2, width), BF16),
            pltpu.VMEM((2, chips, 2, width), BF16),
            pltpu.VMEM((chips, 2, width), BF16),
            pltpu.VMEM((chips, 2, width), F32),
            pltpu.VMEM((chips, 2, 2, width), F32),
            pltpu.VMEM((chips, 2, 2, width), F32),
            pltpu.VMEM((nrep, owned // nrep, width), F32),
            pltpu.VMEM((nrep, owned // nrep, width), F32),
            pltpu.SemaphoreType.DMA((7,)),
            pltpu.SemaphoreType.DMA((2,)),
            pltpu.SemaphoreType.DMA((7,)),
            pltpu.SemaphoreType.DMA((7,)),
        ],
        compiler_params=pltpu.CompilerParams(
            collective_id=0, has_side_effects=True, vmem_limit_bytes=63 * 2**20
        ),
        name="parcel_step",
    )(
        bundle_patch_custodian.reshape(1, blocks),
        bundle_patch_ordinal.reshape(1, blocks),
        busy_bundles_per_accelerator,
        ambient_flow_quantities,
        unscaled_kernel_coefficients,
        jnp.transpose(particle_speeds, (1, 0, 2)),
        particle_diameters,
        particle_kelvins,
    )
    return jnp.transpose(moved, (1, 0, 2)), warmed, source


def solution(mesh, ny=4, nz=16):
    both = ("cells", "rep")
    return jax.shard_map(
        functools.partial(per_device, ny, nz, mesh.shape["rep"]),
        mesh=mesh,
        in_specs=(
            P(both, None, None),
            P(both, None),
            P(both, None),
            P(both, None, None),
            P(both),
            P(both),
            P(both),
            P("cells", None),
        ),
        out_specs=(P(both, None, None), P(both, None), P(both, None)),
        check_vma=False,
    )
```

```python
import functools
import math

import jax
import jax.numpy as jnp
from jax import lax
from jax.experimental import pallas as pl
from jax.experimental.pallas import tpu as pltpu
from jax.sharding import PartitionSpec as P

MESH = pl.DeviceIdType.MESH
F32, BF16, I32, I16 = jnp.float32, jnp.bfloat16, jnp.int32, jnp.int16

REYNOLDS_SCALE = 20.0
DRAG_SCALE = 1.0
HEAT_SCALE = 0.5
PRANDTL_ROOT = 0.9
LOADING = 0.2
ABSENT = 1.0e9
LARGEST = 512.0
OCTAVES = 32
CODES = 1023.5


def iota(shape, axis):
    return lax.broadcasted_iota(I32, shape, axis)


def to_row(column):
    n = column.shape[0]
    eye = iota((n, n), 0) == iota((n, n), 1)
    return jnp.sum(jnp.where(eye, column, 0.0), axis=0, keepdims=True)


def to_column(row):
    n = row.shape[1]
    eye = iota((n, n), 0) == iota((n, n), 1)
    return jnp.sum(jnp.where(eye, row, 0.0), axis=1, keepdims=True)


def halves(x):
    high = x.astype(BF16)
    return high, (x - high.astype(F32)).astype(BF16)


def encode(x):
    least = LARGEST / 2.0**OCTAVES
    code = jnp.log(1.0 + jnp.abs(x) * (1.0 / least)) * (CODES / math.log(2.0))
    code = jnp.where(x < 0.0, -code, code)
    return jnp.round(code).astype(I32).astype(I16)


def decode(code):
    least = LARGEST / 2.0**OCTAVES
    code = code.astype(I32).astype(F32)
    size = jnp.exp(jnp.abs(code) * (math.log(2.0) / CODES)) * least - least
    return jnp.where(code < 0.0, -size, size)


def dot(a, b):
    return jnp.dot(a, b, preferred_element_type=F32)


def step_kernel(
    ny,
    nz,
    nrep,
    owner_hbm,
    place_hbm,
    busy_ref,
    field_hbm,
    tiles_hbm,
    speed_hbm,
    size_hbm,
    heat_hbm,
    moved_hbm,
    warmed_hbm,
    source_ref,
    owner_v,
    place_v,
    field_v,
    tiles,
    speed,
    size,
    heat,
    moved,
    warmed,
    field_x,
    lab_all,
    lab_x,
    row_s,
    row_r,
    sums_x,
    sums_s,
    sums_r,
    part_s,
    part_r,
    in_sem,
    out_sem,
    send_sem,
    recv_sem,
):
    blocks, cells, parcels = tiles.shape
    width = 4 * cells
    owned = field_v.shape[0]
    chips = ny * nz
    sources = 2 * chips
    slots = 2 * sources
    me = lax.axis_index("cells")
    r = lax.axis_index("rep")
    core = me & 1
    chip = me >> 1
    z = chip & (nz - 1)
    y = chip // nz
    steps = sorted(
        ((dy, dz) for dy in range(ny) for dz in range(nz) if dy or dz),
        key=lambda step: (
            -min(step[0], ny - step[0]) - min(step[1], nz - step[1]),
            step,
        ),
    )
    others = []
    for dy, dz in steps:
        other = ((y + dy) & (ny - 1)) * nz + ((z + dz) & (nz - 1))
        others.append((other, {"cells": other * 2 + core, "rep": r}))
    sibling = {"cells": chip * 2 + (1 - core), "rep": r}
    reps = []
    for step in range(1, nrep):
        other = (r + step) & (nrep - 1)
        reps.append((other, {"cells": me, "rep": other}))

    inputs = [
        pltpu.make_async_copy(src, dst, in_sem.at[i])
        for i, (src, dst) in enumerate(
            (
                (owner_hbm, owner_v),
                (place_hbm, place_v),
                (field_hbm, field_v),
                (tiles_hbm, tiles),
                (speed_hbm, speed),
                (size_hbm, size),
                (heat_hbm, heat),
            )
        )
    ]
    for copy in inputs:
        copy.start()

    barrier = pltpu.get_barrier_semaphore()
    for device in [device for _, device in others + reps] + [sibling]:
        pl.semaphore_signal(barrier, inc=1, device_id=device, device_id_type=MESH)

    def send(phase, src, dst, device):
        copy = pltpu.make_async_remote_copy(
            src_ref=src,
            dst_ref=dst,
            send_sem=send_sem.at[phase],
            recv_sem=recv_sem.at[phase],
            device_id=device,
            device_id_type=MESH,
        )
        copy.start()
        return copy

    def arrived(phase, some):
        pltpu.make_async_remote_copy(
            src_ref=some,
            dst_ref=some,
            send_sem=send_sem.at[phase],
            recv_sem=recv_sem.at[phase],
            device_id=sibling,
            device_id_type=MESH,
        ).wait()

    target = iota((1, 8 * cells), 1)
    target = (target // (2 * cells)) * cells + (target & (cells - 1))
    spread = jnp.where(iota((width, 8 * cells), 0) == target, 1.0, 0.0).astype(BF16)
    diagonal = (iota((1, 8 * cells), 1) // cells) == iota((8, 1), 0)
    slot_line = iota((slots, 1), 0)
    pair_line = iota((sources, 1), 0)

    inputs[0].wait()
    inputs[1].wait()
    owner = owner_v[...]
    live = iota((1, blocks), 1) < busy_ref[0]
    label = jnp.where(live, owner * owned + place_v[...], -1)
    lab_all[chip] = label

    ownerf = owner.astype(F32)
    earlier = (
        (to_column(ownerf) == ownerf)
        & (iota((blocks, blocks), 0) < iota((blocks, blocks), 1))
        & (iota((blocks, blocks), 0) < busy_ref[0])
    )
    rank = jnp.sum(jnp.where(earlier, 1.0, 0.0), axis=0, keepdims=True).astype(I32)
    slot = jnp.where((owner & 1) == core, 0, sources) + (owner >> 1) * 2 + rank
    slot = jnp.where(live, slot, -1)
    slot_column = to_column(slot.astype(F32))
    to_slots = jnp.where(slot_line == slot, 1.0, 0.0).astype(BF16)
    from_slots = jnp.where(
        iota((1, slots), 1).astype(F32) == slot_column, 1.0, 0.0
    ).astype(BF16)

    pl.semaphore_wait(barrier, chips - 1 + nrep - 1 + 1)

    for other, device in others:
        send(0, lab_all.at[chip], lab_all.at[chip], device)
    inputs[2].wait()
    fields = send(1, field_v, field_x, sibling)

    def find(table, owner_id):
        place = table[...].reshape(chips, blocks) - owner_id * owned
        match = (place >= 0) & (place < owned)
        key = (iota((chips, blocks), 1) * owned + place).astype(F32)
        first = jnp.min(jnp.where(match, key, ABSENT), axis=1, keepdims=True)
        last = jnp.max(jnp.where(match, key, -1.0), axis=1, keepdims=True)
        size_f = float(owned)
        place_0 = first - jnp.floor(first / size_f) * size_f
        place_1 = last - jnp.floor(last / size_f) * size_f
        return (
            jnp.where(first < ABSENT, place_0, -1.0),
            jnp.where(last > first, place_1, -1.0),
        )

    arrived(0, lab_all.at[pl.ds(0, chips - 1)])
    labels = send(2, lab_all, lab_x, sibling)

    found = [find(lab_all, me), find(lab_all, chip * 2 + (1 - core))]
    fields.wait()
    for i, (places, field) in enumerate(zip(found, (field_v, field_x))):
        wanted = jnp.sum(
            jnp.where(
                iota((1, chips), 1) == (pair_line >> 1),
                jnp.where((pair_line & 1) == 0, to_row(places[0]), to_row(places[1])),
                0.0,
            ),
            axis=1,
            keepdims=True,
        )
        picks = jnp.where(iota((1, owned), 1).astype(F32) == wanted, 1.0, 0.0)
        rows = dot(picks.astype(BF16), field[...]).astype(BF16)
        row_s[i] = rows.reshape(chips, 2, width)
    for other, device in others:
        send(3, row_s.at[:, other], row_r.at[:, chip], device)
    row_r[:, chip] = row_s[:, chip]

    labels.wait()
    lane = iota((1, slots), 1)
    here, there = found[0], find(lab_x, me)
    given = jnp.where(
        (lane & 2) == 0,
        jnp.where((lane & 1) == 0, here[0], here[1]),
        jnp.where((lane & 1) == 0, there[0], there[1]),
    )
    given = jnp.sum(
        jnp.where(iota((chips, 1), 0) == (lane >> 2), given, 0.0), axis=0, keepdims=True
    )
    deposits = jnp.where(iota((owned, 1), 0).astype(F32) == given, 1.0, 0.0).astype(BF16)
    arrived(3, row_r.at[:, pl.ds(0, chips - 1)])

    gas = dot(from_slots, row_r[...].reshape(slots, width))
    gas = dot(gas.astype(BF16), spread)
    for copy in inputs[3:]:
        copy.wait()
    pair = 2 * cells
    sampled = []
    for g in range(blocks // 8):
        left = []
        for c in range(4):
            piece = gas[8 * g : 8 * g + 8, c * pair : (c + 1) * pair]
            left.append(
                jnp.where(diagonal, jnp.concatenate([piece] * 4, axis=1), 0.0)
            )
        left = jnp.concatenate(left, axis=0).astype(BF16)
        sampled.append(
            dot(left, tiles[8 * g : 8 * g + 8].reshape(8 * cells, parcels))
        )
    scale = 2.0 / cells
    u = [
        jnp.concatenate([s[8 * c : 8 * c + 8] for s in sampled], axis=0) * scale
        for c in range(4)
    ]

    v = [speed[c] for c in range(3)]
    d = size[...]
    t = heat[...]
    slip = [u[c] - v[c] for c in range(3)]
    slip_speed = jnp.sqrt(
        1.0 + (slip[0] * slip[0] + slip[1] * slip[1] + slip[2] * slip[2])
    )
    reynolds = REYNOLDS_SCALE * d * slip_speed
    squared = d * d
    drag = DRAG_SCALE * (1.0 + 0.15 * jnp.exp(0.687 * jnp.log(reynolds))) / squared
    warm = HEAT_SCALE * (2.0 + 0.6 * PRANDTL_ROOT * jnp.sqrt(reynolds)) / squared
    mass = LOADING * d * squared
    live_column = slot_column >= 0.0
    terms = []
    for c in range(3):
        new = (v[c] + drag * u[c]) / (1.0 + drag)
        terms.append((-mass * (new - v[c])).astype(BF16))
        moved[c] = jnp.where(live_column, new, v[c])
    new = (t + warm * u[3]) / (1.0 + warm)
    terms.append((-mass * (new - t)).astype(BF16))
    warmed[...] = jnp.where(live_column, new, t)
    outputs = [
        pltpu.make_async_copy(src, dst, out_sem.at[i])
        for i, (src, dst) in enumerate(((moved, moved_hbm), (warmed, warmed_hbm)))
    ]
    for copy in outputs:
        copy.start()

    lane, line = iota((32, pair), 1), iota((32, pair), 0)
    line = line & 7
    low = iota((8, pair), 1) < cells
    rows = []
    termf = [x.astype(F32) for x in terms]
    for g in range(blocks // 8):
        left = jnp.concatenate([x[8 * g : 8 * g + 8] for x in termf], axis=0)
        full = lax.dot_general(
            left.astype(BF16),
            tiles[8 * g : 8 * g + 8].reshape(8 * cells, parcels),
            (((1,), (1,)), ((), ())),
            preferred_element_type=F32,
        )
        own = jnp.zeros((32, pair), F32)
        for j in range(4):
            keep = line == 2 * j + lane // cells
            own = own + jnp.where(keep, full[:, j * pair : (j + 1) * pair], 0.0)
        own = own + pltpu.roll(own, cells, axis=1)
        rows.append(
            jnp.concatenate(
                [
                    jnp.where(low, own[0:8], own[8:16]),
                    jnp.where(low, own[16:24], own[24:32]),
                ],
                axis=1,
            )
        )
    high, rest = halves(jnp.concatenate(rows, axis=0) * scale)

    leave = to_slots[sources:]
    sums_x[...] = encode(dot(leave, high) + dot(leave, rest)).reshape(chips, 2, width)
    copy = send(4, sums_x, sums_s.at[:, 1], sibling)
    stay = to_slots[:sources]
    sums_s[:, 0] = encode(dot(stay, high) + dot(stay, rest)).reshape(chips, 2, width)
    copy.wait()
    for other, device in others:
        send(5, sums_s.at[other], sums_r.at[chip], device)
    sums_r[chip] = sums_s[chip]
    arrived(5, sums_r.at[pl.ds(0, chips - 1)])

    high, rest = halves(decode(sums_r[...].reshape(slots, width)))
    total = dot(deposits, high) + dot(deposits, rest)
    part_s[...] = total.reshape(nrep, owned // nrep, width)
    for other, device in reps:
        send(6, part_s.at[other], part_r.at[r], device)
    part_r[r] = part_s[r]
    arrived(6, part_r.at[pl.ds(0, nrep - 1)])
    total = part_r[0]
    for k in range(1, nrep):
        total = total + part_r[k]
    source_ref[...] = total
    for copy in outputs:
        copy.wait()


def hand_over(count, *refs):
    copies = [
        pltpu.make_async_copy(refs[i], refs[count + i], refs[2 * count].at[i])
        for i in range(count)
    ]
    for copy in copies:
        copy.start()
    for copy in copies:
        copy.wait()


def per_device(
    ny,
    nz,
    nrep,
    particle_speeds,
    particle_diameters,
    particle_kelvins,
    unscaled_kernel_coefficients,
    bundle_patch_ordinal,
    bundle_patch_custodian,
    busy_bundles_per_accelerator,
    ambient_flow_quantities,
):
    blocks, cells, parcels = unscaled_kernel_coefficients.shape
    owned, width = ambient_flow_quantities.shape
    chips = ny * nz
    hbm = pl.BlockSpec(memory_space=pltpu.HBM)
    vmem = pl.BlockSpec(memory_space=pltpu.VMEM)
    smem = pl.BlockSpec(memory_space=pltpu.SMEM)
    results = pl.pallas_call(
        functools.partial(step_kernel, ny, nz, nrep),
        out_shape=(
            jax.ShapeDtypeStruct((3, blocks, parcels), F32),
            jax.ShapeDtypeStruct((blocks, parcels), F32),
            jax.ShapeDtypeStruct((owned // nrep, width), F32),
        ),
        in_specs=[hbm, hbm, smem] + [hbm] * 5,
        out_specs=(hbm, hbm, vmem),
        scratch_shapes=[
            pltpu.VMEM((1, blocks), I32),
            pltpu.VMEM((1, blocks), I32),
            pltpu.VMEM((owned, width), BF16),
            pltpu.VMEM((blocks, cells, parcels), BF16),
            pltpu.VMEM((3, blocks, parcels), F32),
            pltpu.VMEM((blocks, parcels), F32),
            pltpu.VMEM((blocks, parcels), F32),
            pltpu.VMEM((3, blocks, parcels), F32),
            pltpu.VMEM((blocks, parcels), F32),
            pltpu.VMEM((owned, width), BF16),
            pltpu.VMEM((chips, 1, blocks), I32),
            pltpu.VMEM((chips, 1, blocks), I32),
            pltpu.VMEM((2, chips, 2, width), BF16),
            pltpu.VMEM((2, chips, 2, width), BF16),
            pltpu.VMEM((chips, 2, width), I16),
            pltpu.VMEM((chips, 2, 2, width), I16),
            pltpu.VMEM((chips, 2, 2, width), I16),
            pltpu.VMEM((nrep, owned // nrep, width), F32),
            pltpu.VMEM((nrep, owned // nrep, width), F32),
            pltpu.SemaphoreType.DMA((7,)),
            pltpu.SemaphoreType.DMA((2,)),
            pltpu.SemaphoreType.DMA((7,)),
            pltpu.SemaphoreType.DMA((7,)),
        ],
        compiler_params=pltpu.CompilerParams(
            collective_id=0, has_side_effects=True, vmem_limit_bytes=63 * 2**20
        ),
        name="parcel_step",
    )(
        bundle_patch_custodian.reshape(1, blocks),
        bundle_patch_ordinal.reshape(1, blocks),
        busy_bundles_per_accelerator,
        ambient_flow_quantities,
        unscaled_kernel_coefficients,
        jnp.transpose(particle_speeds, (1, 0, 2)),
        particle_diameters,
        particle_kelvins,
    )
    moved, warmed, source = pl.pallas_call(
        functools.partial(hand_over, 3),
        out_shape=tuple(jax.ShapeDtypeStruct(x.shape, x.dtype) for x in results),
        in_specs=[hbm] * 3,
        out_specs=(hbm, hbm, hbm),
        scratch_shapes=[pltpu.SemaphoreType.DMA((3,))],
        compiler_params=pltpu.CompilerParams(vmem_limit_bytes=63 * 2**20),
        name="hand_over",
    )(*results)
    return jnp.transpose(moved, (1, 0, 2)), warmed, source


def solution(mesh, ny=4, nz=16):
    both = ("cells", "rep")
    return jax.shard_map(
        functools.partial(per_device, ny, nz, mesh.shape["rep"]),
        mesh=mesh,
        in_specs=(
            P(both, None, None),
            P(both, None),
            P(both, None),
            P(both, None, None),
            P(both),
            P(both),
            P(both),
            P("cells", None),
        ),
        out_specs=(P(both, None, None), P(both, None), P(both, None)),
        check_vma=False,
    )
```

```python
import functools
import math

import jax
import jax.numpy as jnp
from jax import lax
from jax.experimental import pallas as pl
from jax.experimental.pallas import tpu as pltpu
from jax.sharding import PartitionSpec as P

MESH = pl.DeviceIdType.MESH
F32, BF16, I32, I16 = jnp.float32, jnp.bfloat16, jnp.int32, jnp.int16

REYNOLDS_SCALE = 20.0
DRAG_SCALE = 1.0
HEAT_SCALE = 0.5
PRANDTL_ROOT = 0.9
LOADING = 0.2
ABSENT = 1.0e9
LARGEST = 512.0
OCTAVES = 32
CODES = 1023.5


def iota(shape, axis):
    return lax.broadcasted_iota(I32, shape, axis)


def to_row(column):
    n = column.shape[0]
    eye = iota((n, n), 0) == iota((n, n), 1)
    return jnp.sum(jnp.where(eye, column, 0.0), axis=0, keepdims=True)


def to_column(row):
    n = row.shape[1]
    eye = iota((n, n), 0) == iota((n, n), 1)
    return jnp.sum(jnp.where(eye, row, 0.0), axis=1, keepdims=True)


def halves(x):
    high = x.astype(BF16)
    return high, (x - high.astype(F32)).astype(BF16)


def encode(x):
    least = LARGEST / 2.0**OCTAVES
    code = jnp.log(1.0 + jnp.abs(x) * (1.0 / least)) * (CODES / math.log(2.0))
    return jnp.round(jnp.where(x < 0.0, -code, code))


def decode(code):
    least = LARGEST / 2.0**OCTAVES
    code = code.astype(I32).astype(F32)
    size = jnp.exp(jnp.abs(code) * (math.log(2.0) / CODES)) * least - least
    return jnp.where(code < 0.0, -size, size)


def dot(a, b):
    return jnp.dot(a, b, preferred_element_type=F32)


def step_kernel(
    ny,
    nz,
    nrep,
    owner_hbm,
    place_hbm,
    busy_ref,
    field_hbm,
    tiles_hbm,
    speed_hbm,
    size_hbm,
    heat_hbm,
    moved_hbm,
    warmed_hbm,
    source_ref,
    owner_v,
    place_v,
    field_v,
    tiles,
    speed,
    size,
    heat,
    moved,
    warmed,
    field_x,
    lab_all,
    lab_x,
    row_s,
    row_r,
    sums_x,
    sums_s,
    sums_r,
    part_s,
    part_r,
    in_sem,
    out_sem,
    send_sem,
    recv_sem,
):
    blocks, cells, parcels = tiles.shape
    width = 4 * cells
    owned = field_v.shape[0]
    chips = ny * nz
    sources = 2 * chips
    slots = 2 * sources
    me = lax.axis_index("cells")
    r = lax.axis_index("rep")
    core = me & 1
    chip = me >> 1
    z = chip & (nz - 1)
    y = chip // nz
    steps = sorted(
        ((dy, dz) for dy in range(ny) for dz in range(nz) if dy or dz),
        key=lambda step: (
            -min(step[0], ny - step[0]) - min(step[1], nz - step[1]),
            step,
        ),
    )
    others = []
    for dy, dz in steps:
        other = ((y + dy) & (ny - 1)) * nz + ((z + dz) & (nz - 1))
        others.append((other, {"cells": other * 2 + core, "rep": r}))
    sibling = {"cells": chip * 2 + (1 - core), "rep": r}
    reps = []
    for step in range(1, nrep):
        other = (r + step) & (nrep - 1)
        reps.append((other, {"cells": me, "rep": other}))

    inputs = [
        pltpu.make_async_copy(src, dst, in_sem.at[i])
        for i, (src, dst) in enumerate(
            (
                (owner_hbm, owner_v),
                (place_hbm, place_v),
                (field_hbm, field_v),
                (tiles_hbm, tiles),
                (speed_hbm, speed),
                (size_hbm, size),
                (heat_hbm, heat),
            )
        )
    ]
    for copy in inputs[:3]:
        copy.start()

    barrier = pltpu.get_barrier_semaphore()
    for device in [device for _, device in others + reps] + [sibling]:
        pl.semaphore_signal(barrier, inc=1, device_id=device, device_id_type=MESH)
    for copy in inputs[3:]:
        copy.start()

    def send(phase, src, dst, device):
        copy = pltpu.make_async_remote_copy(
            src_ref=src,
            dst_ref=dst,
            send_sem=send_sem.at[phase],
            recv_sem=recv_sem.at[phase],
            device_id=device,
            device_id_type=MESH,
        )
        copy.start()
        return copy

    def arrived(phase, some):
        pltpu.make_async_remote_copy(
            src_ref=some,
            dst_ref=some,
            send_sem=send_sem.at[phase],
            recv_sem=recv_sem.at[phase],
            device_id=sibling,
            device_id_type=MESH,
        ).wait()

    target = iota((1, 8 * cells), 1)
    target = (target // (2 * cells)) * cells + (target & (cells - 1))
    spread = jnp.where(iota((width, 8 * cells), 0) == target, 1.0, 0.0).astype(BF16)
    diagonal = (iota((1, 8 * cells), 1) // cells) == iota((8, 1), 0)
    slot_line = iota((slots, 1), 0)

    inputs[0].wait()
    inputs[1].wait()
    owner = owner_v[...]
    live = iota((1, blocks), 1) < busy_ref[0]
    label = jnp.where(live, owner * owned + place_v[...], -1)
    lab_all[chip] = label

    ownerf = owner.astype(F32)
    earlier = (
        (to_column(ownerf) == ownerf)
        & (iota((blocks, blocks), 0) < iota((blocks, blocks), 1))
        & (iota((blocks, blocks), 0) < busy_ref[0])
    )
    rank = jnp.sum(jnp.where(earlier, 1.0, 0.0), axis=0, keepdims=True).astype(I32)
    slot = jnp.where((owner & 1) == core, 0, sources) + (owner >> 1) * 2 + rank
    slot = jnp.where(live, slot, -1)
    slot_column = to_column(slot.astype(F32))
    to_slots = jnp.where(slot_line == slot, 1.0, 0.0).astype(BF16)
    from_slots = jnp.where(
        iota((1, slots), 1).astype(F32) == slot_column, 1.0, 0.0
    ).astype(BF16)

    pl.semaphore_wait(barrier, chips - 1 + nrep - 1 + 1)

    for other, device in others:
        send(0, lab_all.at[chip], lab_all.at[chip], device)
    inputs[2].wait()
    fields = send(1, field_v, field_x, sibling)

    second = (iota((sources, blocks), 0) & 1) == 1
    key_lane = iota((sources, blocks), 1) * owned

    def spread_out(table):
        return jnp.broadcast_to(table[...], (chips, 2, blocks)).reshape(sources, blocks)

    def find(labels, owner_id):
        place = labels - owner_id * owned
        match = (place >= 0) & (place < owned)
        key = (key_lane + place).astype(F32)
        key = jnp.where(match, jnp.where(second, -key, key), ABSENT)
        key = jnp.abs(jnp.min(key, axis=1, keepdims=True))
        return key - jnp.floor(key * (1.0 / owned)) * owned

    arrived(0, lab_all.at[pl.ds(0, chips - 1)])
    labels = send(2, lab_all, lab_x, sibling)

    table = spread_out(lab_all)
    field_lane = iota((1, owned), 1).astype(F32)

    def serve(i, place, field):
        picks = jnp.where(field_lane == place, 1.0, 0.0).astype(BF16)
        row_s[i] = dot(picks, field[...]).astype(BF16).reshape(chips, 2, width)
        for other, device in others:
            send(3 + i, row_s.at[i, other], row_r.at[i, chip], device)
        row_r[i, chip] = row_s[i, chip]

    here = find(table, me)
    serve(0, here, field_v)
    place = find(table, chip * 2 + (1 - core))
    fields.wait()
    serve(1, place, field_x)

    labels.wait()
    deposits = []
    for place in (here, find(spread_out(lab_x), me)):
        deposits.append(
            jnp.where(
                iota((owned, 1), 0).astype(F32) == to_row(place), 1.0, 0.0
            ).astype(BF16)
        )
    for i in range(2):
        arrived(3 + i, row_r.at[i, pl.ds(0, chips - 1)])

    gas = dot(from_slots, row_r[...].reshape(slots, width))
    gas = dot(gas.astype(BF16), spread)
    for copy in inputs[3:]:
        copy.wait()
    pair = 2 * cells
    sampled = []
    for g in range(blocks // 8):
        left = []
        for c in range(4):
            piece = gas[8 * g : 8 * g + 8, c * pair : (c + 1) * pair]
            left.append(
                jnp.where(diagonal, jnp.concatenate([piece] * 4, axis=1), 0.0)
            )
        left = jnp.concatenate(left, axis=0).astype(BF16)
        sampled.append(
            dot(left, tiles[8 * g : 8 * g + 8].reshape(8 * cells, parcels))
        )
    scale = 2.0 / cells
    u = [
        jnp.concatenate([s[8 * c : 8 * c + 8] for s in sampled], axis=0) * scale
        for c in range(4)
    ]

    v = [speed[c] for c in range(3)]
    d = size[...]
    t = heat[...]
    slip = [u[c] - v[c] for c in range(3)]
    slip_speed = jnp.sqrt(
        1.0 + (slip[0] * slip[0] + slip[1] * slip[1] + slip[2] * slip[2])
    )
    reynolds = REYNOLDS_SCALE * d * slip_speed
    squared = d * d
    drag = DRAG_SCALE * (1.0 + 0.15 * jnp.exp(0.687 * jnp.log(reynolds))) / squared
    warm = HEAT_SCALE * (2.0 + 0.6 * PRANDTL_ROOT * jnp.sqrt(reynolds)) / squared
    mass = LOADING * d * squared
    live_column = slot_column >= 0.0
    terms = []
    for c in range(3):
        new = (v[c] + drag * u[c]) / (1.0 + drag)
        terms.append((-mass * (new - v[c])).astype(BF16))
        moved[c] = jnp.where(live_column, new, v[c])
    new = (t + warm * u[3]) / (1.0 + warm)
    terms.append((-mass * (new - t)).astype(BF16))
    warmed[...] = jnp.where(live_column, new, t)
    outputs = [
        pltpu.make_async_copy(src, dst, out_sem.at[i])
        for i, (src, dst) in enumerate(((moved, moved_hbm), (warmed, warmed_hbm)))
    ]
    for copy in outputs:
        copy.start()

    lane, line = iota((32, pair), 1), iota((32, pair), 0)
    line = line & 7
    low = iota((8, pair), 1) < cells
    rows = []
    termf = [x.astype(F32) for x in terms]
    for g in range(blocks // 8):
        left = jnp.concatenate([x[8 * g : 8 * g + 8] for x in termf], axis=0)
        full = lax.dot_general(
            left.astype(BF16),
            tiles[8 * g : 8 * g + 8].reshape(8 * cells, parcels),
            (((1,), (1,)), ((), ())),
            preferred_element_type=F32,
        )
        own = jnp.zeros((32, pair), F32)
        for j in range(4):
            keep = line == 2 * j + lane // cells
            own = own + jnp.where(keep, full[:, j * pair : (j + 1) * pair], 0.0)
        own = own + pltpu.roll(own, cells, axis=1)
        rows.append(
            jnp.concatenate(
                [
                    jnp.where(low, own[0:8], own[8:16]),
                    jnp.where(low, own[16:24], own[24:32]),
                ],
                axis=1,
            )
        )
    code = encode(jnp.concatenate(rows, axis=0) * scale)
    high = jnp.floor(code * (1.0 / 256.0)) * 256.0
    code = [high.astype(BF16), (code - high).astype(BF16)]

    def in_slots(lines):
        code_there = dot(lines, code[0]) + dot(lines, code[1])
        return code_there.astype(I32).astype(I16).reshape(chips, 2, width)

    sums_x[...] = in_slots(to_slots[sources:])
    copy = send(5, sums_x, sums_s.at[1], sibling)
    sums_s[0] = in_slots(to_slots[:sources])
    for i in range(2):
        if i == 1:
            copy.wait()
        for other, device in others:
            send(6 + i, sums_s.at[i, other], sums_r.at[i, chip], device)
        sums_r[i, chip] = sums_s[i, chip]

    total = jnp.zeros((owned, width), F32)
    for i in range(2):
        arrived(6 + i, sums_r.at[i, pl.ds(0, chips - 1)])
        high, rest = halves(decode(sums_r[i].reshape(sources, width)))
        total = total + dot(deposits[i], high) + dot(deposits[i], rest)
    part_s[...] = total.reshape(nrep, owned // nrep, width)
    for other, device in reps:
        send(8, part_s.at[other], part_r.at[r], device)
    part_r[r] = part_s[r]
    arrived(8, part_r.at[pl.ds(0, nrep - 1)])
    total = part_r[0]
    for k in range(1, nrep):
        total = total + part_r[k]
    source_ref[...] = total
    for copy in outputs:
        copy.wait()


def hand_over(count, *refs):
    sources, results, held = (refs[i * count : (i + 1) * count] for i in range(3))
    sem_in, sem_out = refs[3 * count :]
    arrive = [
        pltpu.make_async_copy(sources[i], held[i], sem_in.at[i]) for i in range(count)
    ]
    leave = [
        pltpu.make_async_copy(held[i], results[i], sem_out.at[i]) for i in range(count)
    ]
    for copy in arrive:
        copy.start()
    for i in range(count):
        arrive[i].wait()
        leave[i].start()
    for copy in leave:
        copy.wait()


def per_device(
    ny,
    nz,
    nrep,
    particle_speeds,
    particle_diameters,
    particle_kelvins,
    unscaled_kernel_coefficients,
    bundle_patch_ordinal,
    bundle_patch_custodian,
    busy_bundles_per_accelerator,
    ambient_flow_quantities,
):
    blocks, cells, parcels = unscaled_kernel_coefficients.shape
    owned, width = ambient_flow_quantities.shape
    chips = ny * nz
    hbm = pl.BlockSpec(memory_space=pltpu.HBM)
    vmem = pl.BlockSpec(memory_space=pltpu.VMEM)
    smem = pl.BlockSpec(memory_space=pltpu.SMEM)
    results = pl.pallas_call(
        functools.partial(step_kernel, ny, nz, nrep),
        out_shape=(
            jax.ShapeDtypeStruct((3, blocks, parcels), F32),
            jax.ShapeDtypeStruct((blocks, parcels), F32),
            jax.ShapeDtypeStruct((owned // nrep, width), F32),
        ),
        in_specs=[hbm, hbm, smem] + [hbm] * 5,
        out_specs=(hbm, hbm, vmem),
        scratch_shapes=[
            pltpu.VMEM((1, blocks), I32),
            pltpu.VMEM((1, blocks), I32),
            pltpu.VMEM((owned, width), BF16),
            pltpu.VMEM((blocks, cells, parcels), BF16),
            pltpu.VMEM((3, blocks, parcels), F32),
            pltpu.VMEM((blocks, parcels), F32),
            pltpu.VMEM((blocks, parcels), F32),
            pltpu.VMEM((3, blocks, parcels), F32),
            pltpu.VMEM((blocks, parcels), F32),
            pltpu.VMEM((owned, width), BF16),
            pltpu.VMEM((chips, 1, blocks), I32),
            pltpu.VMEM((chips, 1, blocks), I32),
            pltpu.VMEM((2, chips, 2, width), BF16),
            pltpu.VMEM((2, chips, 2, width), BF16),
            pltpu.VMEM((chips, 2, width), I16),
            pltpu.VMEM((2, chips, 2, width), I16),
            pltpu.VMEM((2, chips, 2, width), I16),
            pltpu.VMEM((nrep, owned // nrep, width), F32),
            pltpu.VMEM((nrep, owned // nrep, width), F32),
            pltpu.SemaphoreType.DMA((7,)),
            pltpu.SemaphoreType.DMA((2,)),
            pltpu.SemaphoreType.DMA((9,)),
            pltpu.SemaphoreType.DMA((9,)),
        ],
        compiler_params=pltpu.CompilerParams(
            collective_id=0, has_side_effects=True, vmem_limit_bytes=63 * 2**20
        ),
        name="parcel_step",
    )(
        bundle_patch_custodian.reshape(1, blocks),
        bundle_patch_ordinal.reshape(1, blocks),
        busy_bundles_per_accelerator,
        ambient_flow_quantities,
        unscaled_kernel_coefficients,
        jnp.transpose(particle_speeds, (1, 0, 2)),
        particle_diameters,
        particle_kelvins,
    )
    moved, warmed, source = pl.pallas_call(
        functools.partial(hand_over, 3),
        out_shape=tuple(jax.ShapeDtypeStruct(x.shape, x.dtype) for x in results),
        in_specs=[hbm] * 3,
        out_specs=(hbm, hbm, hbm),
        scratch_shapes=[pltpu.VMEM(x.shape, x.dtype) for x in results]
        + [pltpu.SemaphoreType.DMA((3,))] * 2,
        compiler_params=pltpu.CompilerParams(vmem_limit_bytes=63 * 2**20),
        name="hand_over",
    )(*results)
    return jnp.transpose(moved, (1, 0, 2)), warmed, source


def solution(mesh, ny=4, nz=16):
    both = ("cells", "rep")
    return jax.shard_map(
        functools.partial(per_device, ny, nz, mesh.shape["rep"]),
        mesh=mesh,
        in_specs=(
            P(both, None, None),
            P(both, None),
            P(both, None),
            P(both, None, None),
            P(both),
            P(both),
            P(both),
            P("cells", None),
        ),
        out_specs=(P(both, None, None), P(both, None), P(both, None)),
        check_vma=False,
    )
```

```python
import functools
import math

import jax
import jax.numpy as jnp
from jax import lax
from jax.experimental import pallas as pl
from jax.experimental.pallas import tpu as pltpu
from jax.sharding import PartitionSpec as P

MESH = pl.DeviceIdType.MESH
F32, BF16, I32, I16 = jnp.float32, jnp.bfloat16, jnp.int32, jnp.int16

REYNOLDS_SCALE = 20.0
DRAG_SCALE = 1.0
HEAT_SCALE = 0.5
PRANDTL_ROOT = 0.9
LOADING = 0.2
ABSENT = 1.0e9
LARGEST = 512.0
OCTAVES = 32
CODES = 1023.5


def iota(shape, axis):
    return lax.broadcasted_iota(I32, shape, axis)


def to_row(column):
    n = column.shape[0]
    eye = iota((n, n), 0) == iota((n, n), 1)
    return jnp.sum(jnp.where(eye, column, 0.0), axis=0, keepdims=True)


def to_column(row):
    n = row.shape[1]
    eye = iota((n, n), 0) == iota((n, n), 1)
    return jnp.sum(jnp.where(eye, row, 0.0), axis=1, keepdims=True)


def halves(x):
    high = x.astype(BF16)
    return high, (x - high.astype(F32)).astype(BF16)


def encode(x):
    least = LARGEST / 2.0**OCTAVES
    code = jnp.log(1.0 + jnp.abs(x) * (1.0 / least)) * (CODES / math.log(2.0))
    return jnp.round(jnp.where(x < 0.0, -code, code))


def decode(code):
    least = LARGEST / 2.0**OCTAVES
    code = code.astype(I32).astype(F32)
    size = jnp.exp(jnp.abs(code) * (math.log(2.0) / CODES)) * least - least
    return jnp.where(code < 0.0, -size, size)


def dot(a, b):
    return jnp.dot(a, b, preferred_element_type=F32)


def step_kernel(
    ny,
    nz,
    nrep,
    owner_hbm,
    place_hbm,
    busy_ref,
    field_hbm,
    tiles_hbm,
    speed_hbm,
    size_hbm,
    heat_hbm,
    moved_hbm,
    warmed_hbm,
    source_ref,
    owner_v,
    place_v,
    field_v,
    tiles,
    speed,
    size,
    heat,
    moved,
    warmed,
    field_x,
    lab_all,
    lab_x,
    row_s,
    row_r,
    sums_x,
    sums_s,
    sums_r,
    part_s,
    part_r,
    in_sem,
    out_sem,
    send_sem,
    recv_sem,
):
    blocks, cells, parcels = tiles.shape
    width = 4 * cells
    owned = field_v.shape[0]
    chips = ny * nz
    sources = 2 * chips
    slots = 2 * sources
    me = lax.axis_index("cells")
    r = lax.axis_index("rep")
    core = me & 1
    chip = me >> 1
    z = chip & (nz - 1)
    y = chip // nz
    steps = sorted(
        ((dy, dz) for dy in range(ny) for dz in range(nz) if dy or dz),
        key=lambda step: (
            -min(step[0], ny - step[0]) - min(step[1], nz - step[1]),
            step,
        ),
    )
    others = []
    for dy, dz in steps:
        other = ((y + dy) & (ny - 1)) * nz + ((z + dz) & (nz - 1))
        others.append((other, {"cells": other * 2 + core, "rep": r}))
    sibling = {"cells": chip * 2 + (1 - core), "rep": r}
    reps = []
    for step in range(1, nrep):
        other = (r + step) & (nrep - 1)
        reps.append((other, {"cells": me, "rep": other}))

    inputs = [
        pltpu.make_async_copy(src, dst, in_sem.at[i])
        for i, (src, dst) in enumerate(
            (
                (owner_hbm, owner_v),
                (place_hbm, place_v),
                (field_hbm, field_v),
                (tiles_hbm, tiles),
                (speed_hbm, speed),
                (size_hbm, size),
                (heat_hbm, heat),
            )
        )
    ]
    for copy in inputs[:3]:
        copy.start()

    barrier = pltpu.get_barrier_semaphore()
    for device in [device for _, device in others + reps] + [sibling]:
        pl.semaphore_signal(barrier, inc=1, device_id=device, device_id_type=MESH)
    for copy in inputs[3:]:
        copy.start()

    def send(phase, src, dst, device):
        copy = pltpu.make_async_remote_copy(
            src_ref=src,
            dst_ref=dst,
            send_sem=send_sem.at[phase],
            recv_sem=recv_sem.at[phase],
            device_id=device,
            device_id_type=MESH,
        )
        copy.start()
        return copy

    def arrived(phase, some):
        pltpu.make_async_remote_copy(
            src_ref=some,
            dst_ref=some,
            send_sem=send_sem.at[phase],
            recv_sem=recv_sem.at[phase],
            device_id=sibling,
            device_id_type=MESH,
        ).wait()

    target = iota((1, 8 * cells), 1)
    target = (target // (2 * cells)) * cells + (target & (cells - 1))
    spread = jnp.where(iota((width, 8 * cells), 0) == target, 1.0, 0.0).astype(BF16)
    diagonal = (iota((1, 8 * cells), 1) // cells) == iota((8, 1), 0)
    slot_line = iota((slots, 1), 0)

    inputs[0].wait()
    inputs[1].wait()
    owner = owner_v[...]
    live = iota((1, blocks), 1) < busy_ref[0]
    label = jnp.where(live, owner * owned + place_v[...], -1)
    lab_all[chip] = label

    ownerf = owner.astype(F32)
    earlier = (
        (to_column(ownerf) == ownerf)
        & (iota((blocks, blocks), 0) < iota((blocks, blocks), 1))
        & (iota((blocks, blocks), 0) < busy_ref[0])
    )
    rank = jnp.sum(jnp.where(earlier, 1.0, 0.0), axis=0, keepdims=True).astype(I32)
    slot = jnp.where((owner & 1) == core, 0, sources) + (owner >> 1) * 2 + rank
    slot = jnp.where(live, slot, -1)
    slot_column = to_column(slot.astype(F32))
    to_slots = jnp.where(slot_line == slot, 1.0, 0.0).astype(BF16)
    from_slots = jnp.where(
        iota((1, slots), 1).astype(F32) == slot_column, 1.0, 0.0
    ).astype(BF16)

    pl.semaphore_wait(barrier, chips - 1 + nrep - 1 + 1)

    for other, device in others:
        send(0, lab_all.at[chip], lab_all.at[chip], device)
    inputs[2].wait()
    fields = send(1, field_v, field_x, sibling)

    second = (iota((sources, blocks), 0) & 1) == 1
    key_lane = iota((sources, blocks), 1) * owned

    def spread_out(table):
        return jnp.broadcast_to(table[...], (chips, 2, blocks)).reshape(sources, blocks)

    def find(labels, owner_id):
        place = labels - owner_id * owned
        match = (place >= 0) & (place < owned)
        key = (key_lane + place).astype(F32)
        key = jnp.where(match, jnp.where(second, -key, key), ABSENT)
        key = jnp.abs(jnp.min(key, axis=1, keepdims=True))
        return key - jnp.floor(key * (1.0 / owned)) * owned

    arrived(0, lab_all.at[pl.ds(0, chips - 1)])
    labels = send(2, lab_all, lab_x, sibling)

    table = spread_out(lab_all)
    field_lane = iota((1, owned), 1).astype(F32)

    here = find(table, me)
    place = find(table, chip * 2 + (1 - core))
    fields.wait()
    for i, (wanted, field) in enumerate(((here, field_v), (place, field_x))):
        picks = jnp.where(field_lane == wanted, 1.0, 0.0).astype(BF16)
        row_s[i] = dot(picks, field[...]).astype(BF16).reshape(chips, 2, width)
    for other, device in others:
        send(3, row_s.at[:, other], row_r.at[:, chip], device)
    row_r[:, chip] = row_s[:, chip]

    labels.wait()
    deposits = []
    for place in (here, find(spread_out(lab_x), me)):
        deposits.append(
            jnp.where(
                iota((owned, 1), 0).astype(F32) == to_row(place), 1.0, 0.0
            ).astype(BF16)
        )
    arrived(3, row_r.at[:, pl.ds(0, chips - 1)])

    gas = dot(from_slots, row_r[...].reshape(slots, width))
    gas = dot(gas.astype(BF16), spread)
    for copy in inputs[3:]:
        copy.wait()
    pair = 2 * cells
    sampled = []
    for g in range(blocks // 8):
        left = []
        for c in range(4):
            piece = gas[8 * g : 8 * g + 8, c * pair : (c + 1) * pair]
            left.append(
                jnp.where(diagonal, jnp.concatenate([piece] * 4, axis=1), 0.0)
            )
        left = jnp.concatenate(left, axis=0).astype(BF16)
        sampled.append(
            dot(left, tiles[8 * g : 8 * g + 8].reshape(8 * cells, parcels))
        )
    scale = 2.0 / cells
    u = [
        jnp.concatenate([s[8 * c : 8 * c + 8] for s in sampled], axis=0) * scale
        for c in range(4)
    ]

    v = [speed[c] for c in range(3)]
    d = size[...]
    t = heat[...]
    slip = [u[c] - v[c] for c in range(3)]
    slip_speed = jnp.sqrt(
        1.0 + (slip[0] * slip[0] + slip[1] * slip[1] + slip[2] * slip[2])
    )
    reynolds = REYNOLDS_SCALE * d * slip_speed
    squared = d * d
    drag = DRAG_SCALE * (1.0 + 0.15 * jnp.exp(0.687 * jnp.log(reynolds))) / squared
    warm = HEAT_SCALE * (2.0 + 0.6 * PRANDTL_ROOT * jnp.sqrt(reynolds)) / squared
    mass = LOADING * d * squared
    live_column = slot_column >= 0.0
    terms = []
    for c in range(3):
        new = (v[c] + drag * u[c]) / (1.0 + drag)
        terms.append((-mass * (new - v[c])).astype(BF16))
        moved[c] = jnp.where(live_column, new, v[c])
    new = (t + warm * u[3]) / (1.0 + warm)
    terms.append((-mass * (new - t)).astype(BF16))
    warmed[...] = jnp.where(live_column, new, t)
    outputs = [
        pltpu.make_async_copy(src, dst, out_sem.at[i])
        for i, (src, dst) in enumerate(((moved, moved_hbm), (warmed, warmed_hbm)))
    ]
    for copy in outputs:
        copy.start()

    lane, line = iota((32, pair), 1), iota((32, pair), 0)
    line = line & 7
    low = iota((8, pair), 1) < cells
    rows = []
    termf = [x.astype(F32) for x in terms]
    for g in range(blocks // 8):
        left = jnp.concatenate([x[8 * g : 8 * g + 8] for x in termf], axis=0)
        full = lax.dot_general(
            left.astype(BF16),
            tiles[8 * g : 8 * g + 8].reshape(8 * cells, parcels),
            (((1,), (1,)), ((), ())),
            preferred_element_type=F32,
        )
        own = jnp.zeros((32, pair), F32)
        for j in range(4):
            keep = line == 2 * j + lane // cells
            own = own + jnp.where(keep, full[:, j * pair : (j + 1) * pair], 0.0)
        own = own + pltpu.roll(own, cells, axis=1)
        rows.append(
            jnp.concatenate(
                [
                    jnp.where(low, own[0:8], own[8:16]),
                    jnp.where(low, own[16:24], own[24:32]),
                ],
                axis=1,
            )
        )
    code = encode(jnp.concatenate(rows, axis=0) * scale)
    high = jnp.floor(code * (1.0 / 256.0)) * 256.0
    code = [high.astype(BF16), (code - high).astype(BF16)]

    def in_slots(lines):
        code_there = dot(lines, code[0]) + dot(lines, code[1])
        return code_there.astype(I32).astype(I16).reshape(chips, 2, width)

    sums_x[...] = in_slots(to_slots[sources:])
    copy = send(5, sums_x, sums_s.at[1], sibling)
    sums_s[0] = in_slots(to_slots[:sources])
    for i in range(2):
        if i == 1:
            copy.wait()
        for other, device in others:
            send(6 + i, sums_s.at[i, other], sums_r.at[i, chip], device)
        sums_r[i, chip] = sums_s[i, chip]

    total = jnp.zeros((owned, width), F32)
    for i in range(2):
        arrived(6 + i, sums_r.at[i, pl.ds(0, chips - 1)])
        high, rest = halves(decode(sums_r[i].reshape(sources, width)))
        total = total + dot(deposits[i], high) + dot(deposits[i], rest)
    part_s[...] = total.reshape(nrep, owned // nrep, width)
    for other, device in reps:
        send(8, part_s.at[other], part_r.at[r], device)
    part_r[r] = part_s[r]
    arrived(8, part_r.at[pl.ds(0, nrep - 1)])
    total = part_r[0]
    for k in range(1, nrep):
        total = total + part_r[k]
    source_ref[...] = total
    for copy in outputs:
        copy.wait()


def hand_over(count, *refs):
    sources, results, held = (refs[i * count : (i + 1) * count] for i in range(3))
    sem_in, sem_out = refs[3 * count :]
    arrive = [
        pltpu.make_async_copy(sources[i], held[i], sem_in.at[i]) for i in range(count)
    ]
    leave = [
        pltpu.make_async_copy(held[i], results[i], sem_out.at[i]) for i in range(count)
    ]
    for copy in arrive:
        copy.start()
    for i in range(count):
        arrive[i].wait()
        leave[i].start()
    for copy in leave:
        copy.wait()


def per_device(
    ny,
    nz,
    nrep,
    particle_speeds,
    particle_diameters,
    particle_kelvins,
    unscaled_kernel_coefficients,
    bundle_patch_ordinal,
    bundle_patch_custodian,
    busy_bundles_per_accelerator,
    ambient_flow_quantities,
):
    blocks, cells, parcels = unscaled_kernel_coefficients.shape
    owned, width = ambient_flow_quantities.shape
    chips = ny * nz
    hbm = pl.BlockSpec(memory_space=pltpu.HBM)
    vmem = pl.BlockSpec(memory_space=pltpu.VMEM)
    smem = pl.BlockSpec(memory_space=pltpu.SMEM)
    results = pl.pallas_call(
        functools.partial(step_kernel, ny, nz, nrep),
        out_shape=(
            jax.ShapeDtypeStruct((3, blocks, parcels), F32),
            jax.ShapeDtypeStruct((blocks, parcels), F32),
            jax.ShapeDtypeStruct((owned // nrep, width), F32),
        ),
        in_specs=[hbm, hbm, smem] + [hbm] * 5,
        out_specs=(hbm, hbm, vmem),
        scratch_shapes=[
            pltpu.VMEM((1, blocks), I32),
            pltpu.VMEM((1, blocks), I32),
            pltpu.VMEM((owned, width), BF16),
            pltpu.VMEM((blocks, cells, parcels), BF16),
            pltpu.VMEM((3, blocks, parcels), F32),
            pltpu.VMEM((blocks, parcels), F32),
            pltpu.VMEM((blocks, parcels), F32),
            pltpu.VMEM((3, blocks, parcels), F32),
            pltpu.VMEM((blocks, parcels), F32),
            pltpu.VMEM((owned, width), BF16),
            pltpu.VMEM((chips, 1, blocks), I32),
            pltpu.VMEM((chips, 1, blocks), I32),
            pltpu.VMEM((2, chips, 2, width), BF16),
            pltpu.VMEM((2, chips, 2, width), BF16),
            pltpu.VMEM((chips, 2, width), I16),
            pltpu.VMEM((2, chips, 2, width), I16),
            pltpu.VMEM((2, chips, 2, width), I16),
            pltpu.VMEM((nrep, owned // nrep, width), F32),
            pltpu.VMEM((nrep, owned // nrep, width), F32),
            pltpu.SemaphoreType.DMA((7,)),
            pltpu.SemaphoreType.DMA((2,)),
            pltpu.SemaphoreType.DMA((9,)),
            pltpu.SemaphoreType.DMA((9,)),
        ],
        compiler_params=pltpu.CompilerParams(
            collective_id=0, has_side_effects=True, vmem_limit_bytes=63 * 2**20
        ),
        name="parcel_step",
    )(
        bundle_patch_custodian.reshape(1, blocks),
        bundle_patch_ordinal.reshape(1, blocks),
        busy_bundles_per_accelerator,
        ambient_flow_quantities,
        unscaled_kernel_coefficients,
        jnp.transpose(particle_speeds, (1, 0, 2)),
        particle_diameters,
        particle_kelvins,
    )
    moved, warmed, source = pl.pallas_call(
        functools.partial(hand_over, 3),
        out_shape=tuple(jax.ShapeDtypeStruct(x.shape, x.dtype) for x in results),
        in_specs=[hbm] * 3,
        out_specs=(hbm, hbm, hbm),
        scratch_shapes=[pltpu.VMEM(x.shape, x.dtype) for x in results]
        + [pltpu.SemaphoreType.DMA((3,))] * 2,
        compiler_params=pltpu.CompilerParams(vmem_limit_bytes=63 * 2**20),
        name="hand_over",
    )(*results)
    return jnp.transpose(moved, (1, 0, 2)), warmed, source


def solution(mesh, ny=4, nz=16):
    both = ("cells", "rep")
    return jax.shard_map(
        functools.partial(per_device, ny, nz, mesh.shape["rep"]),
        mesh=mesh,
        in_specs=(
            P(both, None, None),
            P(both, None),
            P(both, None),
            P(both, None, None),
            P(both),
            P(both),
            P(both),
            P("cells", None),
        ),
        out_specs=(P(both, None, None), P(both, None), P(both, None)),
        check_vma=False,
    )
```

```python
import functools
import math

import jax
import jax.numpy as jnp
from jax import lax
from jax.experimental import pallas as pl
from jax.experimental.pallas import tpu as pltpu
from jax.sharding import PartitionSpec as P

MESH = pl.DeviceIdType.MESH
F32, BF16, I32, I16 = jnp.float32, jnp.bfloat16, jnp.int32, jnp.int16

REYNOLDS_SCALE = 20.0
DRAG_SCALE = 1.0
HEAT_SCALE = 0.5
PRANDTL_ROOT = 0.9
LOADING = 0.2
ABSENT = 1.0e9
LARGEST = 512.0
OCTAVES = 32
CODES = 1023.5
PART_CODES = 819.0


def iota(shape, axis):
    return lax.broadcasted_iota(I32, shape, axis)


def to_row(column):
    n = column.shape[0]
    eye = iota((n, n), 0) == iota((n, n), 1)
    return jnp.sum(jnp.where(eye, column, 0.0), axis=0, keepdims=True)


def to_column(row):
    n = row.shape[1]
    eye = iota((n, n), 0) == iota((n, n), 1)
    return jnp.sum(jnp.where(eye, row, 0.0), axis=1, keepdims=True)


def halves(x):
    high = x.astype(BF16)
    return high, (x - high.astype(F32)).astype(BF16)


def encode(x, codes=CODES):
    least = LARGEST / 2.0**OCTAVES
    code = jnp.log(1.0 + jnp.abs(x) * (1.0 / least)) * (codes / math.log(2.0))
    return jnp.round(jnp.where(x < 0.0, -code, code))


def decode(code, codes=CODES):
    least = LARGEST / 2.0**OCTAVES
    code = code.astype(I32).astype(F32)
    size = jnp.exp(jnp.abs(code) * (math.log(2.0) / codes)) * least - least
    return jnp.where(code < 0.0, -size, size)


def dot(a, b):
    return jnp.dot(a, b, preferred_element_type=F32)


def step_kernel(
    ny,
    nz,
    nrep,
    owner_hbm,
    place_hbm,
    busy_ref,
    field_hbm,
    tiles_hbm,
    speed_hbm,
    size_hbm,
    heat_hbm,
    moved_hbm,
    warmed_hbm,
    source_ref,
    owner_v,
    place_v,
    field_v,
    tiles,
    speed,
    size,
    heat,
    moved,
    warmed,
    field_x,
    lab_all,
    lab_x,
    row_s,
    row_r,
    sums_x,
    sums_s,
    sums_r,
    part_v,
    part_s,
    part_r,
    in_sem,
    out_sem,
    send_sem,
    recv_sem,
):
    blocks, cells, parcels = tiles.shape
    width = 4 * cells
    owned = field_v.shape[0]
    chips = ny * nz
    sources = 2 * chips
    slots = 2 * sources
    me = lax.axis_index("cells")
    r = lax.axis_index("rep")
    core = me & 1
    chip = me >> 1
    z = chip & (nz - 1)
    y = chip // nz
    steps = sorted(
        ((dy, dz) for dy in range(ny) for dz in range(nz) if dy or dz),
        key=lambda step: (
            -min(step[0], ny - step[0]) - min(step[1], nz - step[1]),
            step,
        ),
    )
    others = []
    for dy, dz in steps:
        other = ((y + dy) & (ny - 1)) * nz + ((z + dz) & (nz - 1))
        others.append((other, {"cells": other * 2 + core, "rep": r}))
    sibling = {"cells": chip * 2 + (1 - core), "rep": r}
    reps = []
    for step in range(1, nrep):
        other = (r + step) & (nrep - 1)
        reps.append((other, {"cells": me, "rep": other}))

    inputs = [
        pltpu.make_async_copy(src, dst, in_sem.at[i])
        for i, (src, dst) in enumerate(
            (
                (owner_hbm, owner_v),
                (place_hbm, place_v),
                (field_hbm, field_v),
                (tiles_hbm, tiles),
                (speed_hbm, speed),
                (size_hbm, size),
                (heat_hbm, heat),
            )
        )
    ]
    for copy in inputs[:3]:
        copy.start()

    barrier = pltpu.get_barrier_semaphore()
    for device in [device for _, device in others + reps] + [sibling]:
        pl.semaphore_signal(barrier, inc=1, device_id=device, device_id_type=MESH)
    for copy in inputs[3:]:
        copy.start()

    def send(phase, src, dst, device):
        copy = pltpu.make_async_remote_copy(
            src_ref=src,
            dst_ref=dst,
            send_sem=send_sem.at[phase],
            recv_sem=recv_sem.at[phase],
            device_id=device,
            device_id_type=MESH,
        )
        copy.start()
        return copy

    def arrived(phase, some):
        pltpu.make_async_remote_copy(
            src_ref=some,
            dst_ref=some,
            send_sem=send_sem.at[phase],
            recv_sem=recv_sem.at[phase],
            device_id=sibling,
            device_id_type=MESH,
        ).wait()

    target = iota((1, 8 * cells), 1)
    target = (target // (2 * cells)) * cells + (target & (cells - 1))
    spread = jnp.where(iota((width, 8 * cells), 0) == target, 1.0, 0.0).astype(BF16)
    diagonal = (iota((1, 8 * cells), 1) // cells) == iota((8, 1), 0)
    slot_line = iota((slots, 1), 0)

    inputs[0].wait()
    inputs[1].wait()
    owner = owner_v[...]
    live = iota((1, blocks), 1) < busy_ref[0]
    label = jnp.where(live, owner * owned + place_v[...], -1)
    lab_all[chip] = label

    ownerf = owner.astype(F32)
    earlier = (
        (to_column(ownerf) == ownerf)
        & (iota((blocks, blocks), 0) < iota((blocks, blocks), 1))
        & (iota((blocks, blocks), 0) < busy_ref[0])
    )
    rank = jnp.sum(jnp.where(earlier, 1.0, 0.0), axis=0, keepdims=True).astype(I32)
    slot = jnp.where((owner & 1) == core, 0, sources) + (owner >> 1) * 2 + rank
    slot = jnp.where(live, slot, -1)
    slot_column = to_column(slot.astype(F32))
    to_slots = jnp.where(slot_line == slot, 1.0, 0.0).astype(BF16)
    from_slots = jnp.where(
        iota((1, slots), 1).astype(F32) == slot_column, 1.0, 0.0
    ).astype(BF16)

    pl.semaphore_wait(barrier, chips - 1 + nrep - 1 + 1)

    for other, device in others:
        send(0, lab_all.at[chip], lab_all.at[chip], device)
    inputs[2].wait()
    fields = send(1, field_v, field_x, sibling)

    second = (iota((sources, blocks), 0) & 1) == 1
    key_lane = iota((sources, blocks), 1) * owned

    def spread_out(table):
        return jnp.broadcast_to(table[...], (chips, 2, blocks)).reshape(sources, blocks)

    def find(labels, owner_id):
        place = labels - owner_id * owned
        match = (place >= 0) & (place < owned)
        key = (key_lane + place).astype(F32)
        key = jnp.where(match, jnp.where(second, -key, key), ABSENT)
        key = jnp.abs(jnp.min(key, axis=1, keepdims=True))
        return key - jnp.floor(key * (1.0 / owned)) * owned

    arrived(0, lab_all.at[pl.ds(0, chips - 1)])
    labels = send(2, lab_all, lab_x, sibling)

    table = spread_out(lab_all)
    field_lane = iota((1, owned), 1).astype(F32)

    here = find(table, me)
    place = find(table, chip * 2 + (1 - core))
    fields.wait()
    for i, (wanted, field) in enumerate(((here, field_v), (place, field_x))):
        picks = jnp.where(field_lane == wanted, 1.0, 0.0).astype(BF16)
        row_s[i] = dot(picks, field[...]).astype(BF16).reshape(chips, 2, width)
    for other, device in others:
        send(3, row_s.at[:, other], row_r.at[:, chip], device)
    row_r[:, chip] = row_s[:, chip]

    labels.wait()
    deposits = []
    for place in (here, find(spread_out(lab_x), me)):
        deposits.append(
            jnp.where(
                iota((owned, 1), 0).astype(F32) == to_row(place), 1.0, 0.0
            ).astype(BF16)
        )
    arrived(3, row_r.at[:, pl.ds(0, chips - 1)])

    gas = dot(from_slots, row_r[...].reshape(slots, width))
    gas = dot(gas.astype(BF16), spread)
    for copy in inputs[3:]:
        copy.wait()
    pair = 2 * cells
    sampled = []
    for g in range(blocks // 8):
        left = []
        for c in range(4):
            piece = gas[8 * g : 8 * g + 8, c * pair : (c + 1) * pair]
            left.append(
                jnp.where(diagonal, jnp.concatenate([piece] * 4, axis=1), 0.0)
            )
        left = jnp.concatenate(left, axis=0).astype(BF16)
        sampled.append(
            dot(left, tiles[8 * g : 8 * g + 8].reshape(8 * cells, parcels))
        )
    scale = 2.0 / cells
    u = [
        jnp.concatenate([s[8 * c : 8 * c + 8] for s in sampled], axis=0) * scale
        for c in range(4)
    ]

    v = [speed[c] for c in range(3)]
    d = size[...]
    t = heat[...]
    slip = [u[c] - v[c] for c in range(3)]
    slip_speed = jnp.sqrt(
        1.0 + (slip[0] * slip[0] + slip[1] * slip[1] + slip[2] * slip[2])
    )
    reynolds = REYNOLDS_SCALE * d * slip_speed
    squared = d * d
    drag = DRAG_SCALE * (1.0 + 0.15 * jnp.exp(0.687 * jnp.log(reynolds))) / squared
    warm = HEAT_SCALE * (2.0 + 0.6 * PRANDTL_ROOT * jnp.sqrt(reynolds)) / squared
    mass = LOADING * d * squared
    live_column = slot_column >= 0.0
    terms = []
    for c in range(3):
        new = (v[c] + drag * u[c]) / (1.0 + drag)
        terms.append((-mass * (new - v[c])).astype(BF16))
        moved[c] = jnp.where(live_column, new, v[c])
    new = (t + warm * u[3]) / (1.0 + warm)
    terms.append((-mass * (new - t)).astype(BF16))
    warmed[...] = jnp.where(live_column, new, t)
    outputs = [
        pltpu.make_async_copy(src, dst, out_sem.at[i])
        for i, (src, dst) in enumerate(((moved, moved_hbm), (warmed, warmed_hbm)))
    ]
    for copy in outputs:
        copy.start()

    lane, line = iota((32, pair), 1), iota((32, pair), 0)
    line = line & 7
    low = iota((8, pair), 1) < cells
    rows = []
    termf = [x.astype(F32) for x in terms]
    for g in range(blocks // 8):
        left = jnp.concatenate([x[8 * g : 8 * g + 8] for x in termf], axis=0)
        full = lax.dot_general(
            left.astype(BF16),
            tiles[8 * g : 8 * g + 8].reshape(8 * cells, parcels),
            (((1,), (1,)), ((), ())),
            preferred_element_type=F32,
        )
        own = jnp.zeros((32, pair), F32)
        for j in range(4):
            keep = line == 2 * j + lane // cells
            own = own + jnp.where(keep, full[:, j * pair : (j + 1) * pair], 0.0)
        own = own + pltpu.roll(own, cells, axis=1)
        rows.append(
            jnp.concatenate(
                [
                    jnp.where(low, own[0:8], own[8:16]),
                    jnp.where(low, own[16:24], own[24:32]),
                ],
                axis=1,
            )
        )
    code = encode(jnp.concatenate(rows, axis=0) * scale)
    high = jnp.floor(code * (1.0 / 256.0)) * 256.0
    code = [high.astype(BF16), (code - high).astype(BF16)]

    def in_slots(lines):
        code_there = dot(lines, code[0]) + dot(lines, code[1])
        return code_there.astype(I32).astype(I16).reshape(chips, 2, width)

    sums_x[...] = in_slots(to_slots[sources:])
    copy = send(5, sums_x, sums_s.at[1], sibling)
    sums_s[0] = in_slots(to_slots[:sources])
    far, near = others[: len(others) // 2], others[len(others) // 2 :]
    for other, device in far:
        send(6, sums_s.at[0, other], sums_r.at[0, chip], device)
    copy.wait()
    for other, device in far:
        send(6, sums_s.at[1, other], sums_r.at[1, chip], device)
    for other, device in near:
        send(6, sums_s.at[:, other], sums_r.at[:, chip], device)
    sums_r[:, chip] = sums_s[:, chip]

    total = jnp.zeros((owned, width), F32)
    arrived(6, sums_r.at[:, pl.ds(0, chips - 1)])
    for i in range(2):
        high, rest = halves(decode(sums_r[i].reshape(sources, width)))
        total = total + dot(deposits[i], high) + dot(deposits[i], rest)
    total = total.reshape(nrep, owned // nrep, width)
    part_s[...] = encode(total, PART_CODES).astype(I32).astype(I16)
    part_v[...] = total
    for other, device in reps:
        send(8, part_s.at[other], part_r.at[r], device)
    part_r[r] = jnp.zeros(part_r.shape[1:], I16)
    arrived(8, part_r.at[pl.ds(0, nrep - 1)])
    total = part_v[r]
    for k in range(nrep):
        total = total + decode(part_r[k], PART_CODES)
    source_ref[...] = total
    for copy in outputs:
        copy.wait()


def hand_over(count, *refs):
    sources, results, held = (refs[i * count : (i + 1) * count] for i in range(3))
    sem_in, sem_out = refs[3 * count :]
    arrive = [
        pltpu.make_async_copy(sources[i], held[i], sem_in.at[i]) for i in range(count)
    ]
    leave = [
        pltpu.make_async_copy(held[i], results[i], sem_out.at[i]) for i in range(count)
    ]
    for copy in arrive:
        copy.start()
    for i in range(count):
        arrive[i].wait()
        leave[i].start()
    for copy in leave:
        copy.wait()


def per_device(
    ny,
    nz,
    nrep,
    particle_speeds,
    particle_diameters,
    particle_kelvins,
    unscaled_kernel_coefficients,
    bundle_patch_ordinal,
    bundle_patch_custodian,
    busy_bundles_per_accelerator,
    ambient_flow_quantities,
):
    blocks, cells, parcels = unscaled_kernel_coefficients.shape
    owned, width = ambient_flow_quantities.shape
    chips = ny * nz
    hbm = pl.BlockSpec(memory_space=pltpu.HBM)
    vmem = pl.BlockSpec(memory_space=pltpu.VMEM)
    smem = pl.BlockSpec(memory_space=pltpu.SMEM)
    results = pl.pallas_call(
        functools.partial(step_kernel, ny, nz, nrep),
        out_shape=(
            jax.ShapeDtypeStruct((3, blocks, parcels), F32),
            jax.ShapeDtypeStruct((blocks, parcels), F32),
            jax.ShapeDtypeStruct((owned // nrep, width), F32),
        ),
        in_specs=[hbm, hbm, smem] + [hbm] * 5,
        out_specs=(hbm, hbm, vmem),
        scratch_shapes=[
            pltpu.VMEM((1, blocks), I32),
            pltpu.VMEM((1, blocks), I32),
            pltpu.VMEM((owned, width), BF16),
            pltpu.VMEM((blocks, cells, parcels), BF16),
            pltpu.VMEM((3, blocks, parcels), F32),
            pltpu.VMEM((blocks, parcels), F32),
            pltpu.VMEM((blocks, parcels), F32),
            pltpu.VMEM((3, blocks, parcels), F32),
            pltpu.VMEM((blocks, parcels), F32),
            pltpu.VMEM((owned, width), BF16),
            pltpu.VMEM((chips, 1, blocks), I32),
            pltpu.VMEM((chips, 1, blocks), I32),
            pltpu.VMEM((2, chips, 2, width), BF16),
            pltpu.VMEM((2, chips, 2, width), BF16),
            pltpu.VMEM((chips, 2, width), I16),
            pltpu.VMEM((2, chips, 2, width), I16),
            pltpu.VMEM((2, chips, 2, width), I16),
            pltpu.VMEM((nrep, owned // nrep, width), F32),
            pltpu.VMEM((nrep, owned // nrep, width), I16),
            pltpu.VMEM((nrep, owned // nrep, width), I16),
            pltpu.SemaphoreType.DMA((7,)),
            pltpu.SemaphoreType.DMA((2,)),
            pltpu.SemaphoreType.DMA((9,)),
            pltpu.SemaphoreType.DMA((9,)),
        ],
        compiler_params=pltpu.CompilerParams(
            collective_id=0, has_side_effects=True, vmem_limit_bytes=63 * 2**20
        ),
        name="parcel_step",
    )(
        bundle_patch_custodian.reshape(1, blocks),
        bundle_patch_ordinal.reshape(1, blocks),
        busy_bundles_per_accelerator,
        ambient_flow_quantities,
        unscaled_kernel_coefficients,
        jnp.transpose(particle_speeds, (1, 0, 2)),
        particle_diameters,
        particle_kelvins,
    )
    moved, warmed, source = pl.pallas_call(
        functools.partial(hand_over, 3),
        out_shape=tuple(jax.ShapeDtypeStruct(x.shape, x.dtype) for x in results),
        in_specs=[hbm] * 3,
        out_specs=(hbm, hbm, hbm),
        scratch_shapes=[pltpu.VMEM(x.shape, x.dtype) for x in results]
        + [pltpu.SemaphoreType.DMA((3,))] * 2,
        compiler_params=pltpu.CompilerParams(vmem_limit_bytes=63 * 2**20),
        name="hand_over",
    )(*results)
    return jnp.transpose(moved, (1, 0, 2)), warmed, source


def solution(mesh, ny=4, nz=16):
    both = ("cells", "rep")
    return jax.shard_map(
        functools.partial(per_device, ny, nz, mesh.shape["rep"]),
        mesh=mesh,
        in_specs=(
            P(both, None, None),
            P(both, None),
            P(both, None),
            P(both, None, None),
            P(both),
            P(both),
            P(both),
            P("cells", None),
        ),
        out_specs=(P(both, None, None), P(both, None), P(both, None)),
        check_vma=False,
    )
```

```python
import functools
import math

import jax
import jax.numpy as jnp
from jax import lax
from jax.experimental import pallas as pl
from jax.experimental.pallas import tpu as pltpu
from jax.sharding import PartitionSpec as P

MESH = pl.DeviceIdType.MESH
F32, BF16, I32, I16 = jnp.float32, jnp.bfloat16, jnp.int32, jnp.int16

REYNOLDS_SCALE = 20.0
DRAG_SCALE = 1.0
HEAT_SCALE = 0.5
PRANDTL_ROOT = 0.9
LOADING = 0.2
ABSENT = 1.0e9
LARGEST = 512.0
OCTAVES = 32
CODES = 1023.5
PART_CODES = 819.0


def iota(shape, axis):
    return lax.broadcasted_iota(I32, shape, axis)


def to_row(column):
    n = column.shape[0]
    eye = iota((n, n), 0) == iota((n, n), 1)
    return jnp.sum(jnp.where(eye, column, 0.0), axis=0, keepdims=True)


def to_column(row):
    n = row.shape[1]
    eye = iota((n, n), 0) == iota((n, n), 1)
    return jnp.sum(jnp.where(eye, row, 0.0), axis=1, keepdims=True)


def halves(x):
    high = x.astype(BF16)
    return high, (x - high.astype(F32)).astype(BF16)


def encode(x, codes=CODES):
    least = LARGEST / 2.0**OCTAVES
    code = jnp.log(1.0 + jnp.abs(x) * (1.0 / least)) * (codes / math.log(2.0))
    return jnp.round(jnp.where(x < 0.0, -code, code))


def decode(code, codes=CODES):
    least = LARGEST / 2.0**OCTAVES
    code = code.astype(I32).astype(F32)
    size = jnp.exp(jnp.abs(code) * (math.log(2.0) / codes)) * least - least
    return jnp.where(code < 0.0, -size, size)


def dot(a, b):
    return jnp.dot(a, b, preferred_element_type=F32)


def step_kernel(
    ny,
    nz,
    nrep,
    owner_hbm,
    place_hbm,
    busy_ref,
    field_hbm,
    tiles_hbm,
    speed_hbm,
    size_hbm,
    heat_hbm,
    moved_hbm,
    warmed_hbm,
    source_ref,
    owner_v,
    place_v,
    field_v,
    tiles,
    speed,
    size,
    heat,
    moved,
    warmed,
    field_x,
    lab_all,
    lab_x,
    row_s,
    row_r,
    sums_x,
    sums_s,
    sums_r,
    deposits,
    part_s,
    part_r,
    in_sem,
    out_sem,
    send_sem,
    recv_sem,
):
    blocks, cells, parcels = tiles.shape
    width = 4 * cells
    owned = field_v.shape[0]
    chips = ny * nz
    sources = 2 * chips
    slots = 2 * sources
    me = lax.axis_index("cells")
    r = lax.axis_index("rep")
    core = me & 1
    chip = me >> 1
    z = chip & (nz - 1)
    y = chip // nz
    steps = sorted(
        ((dy, dz) for dy in range(ny) for dz in range(nz) if dy or dz),
        key=lambda step: (
            -min(step[0], ny - step[0]) - min(step[1], nz - step[1]),
            step,
        ),
    )
    others = []
    for dy, dz in steps:
        other = ((y + dy) & (ny - 1)) * nz + ((z + dz) & (nz - 1))
        others.append((other, {"cells": other * 2 + core, "rep": r}))
    sibling = {"cells": chip * 2 + (1 - core), "rep": r}
    reps = []
    for step in sorted(range(nrep), key=lambda step: -min(step, nrep - step)):
        other = (r + step) & (nrep - 1)
        reps.append((step, other, {"cells": me, "rep": other}))

    inputs = [
        pltpu.make_async_copy(src, dst, in_sem.at[i])
        for i, (src, dst) in enumerate(
            (
                (owner_hbm, owner_v),
                (place_hbm, place_v),
                (field_hbm, field_v),
                (tiles_hbm, tiles),
                (speed_hbm, speed),
                (size_hbm, size),
                (heat_hbm, heat),
            )
        )
    ]
    for copy in inputs[:3]:
        copy.start()

    barrier = pltpu.get_barrier_semaphore()
    peers = [device for _, device in others] + [device for _, _, device in reps[:-1]]
    for device in peers + [sibling]:
        pl.semaphore_signal(barrier, inc=1, device_id=device, device_id_type=MESH)
    for copy in inputs[3:]:
        copy.start()

    def send(phase, src, dst, device):
        copy = pltpu.make_async_remote_copy(
            src_ref=src,
            dst_ref=dst,
            send_sem=send_sem.at[phase],
            recv_sem=recv_sem.at[phase],
            device_id=device,
            device_id_type=MESH,
        )
        copy.start()
        return copy

    def arrived(phase, some):
        pltpu.make_async_remote_copy(
            src_ref=some,
            dst_ref=some,
            send_sem=send_sem.at[phase],
            recv_sem=recv_sem.at[phase],
            device_id=sibling,
            device_id_type=MESH,
        ).wait()

    target = iota((1, 8 * cells), 1)
    target = (target // (2 * cells)) * cells + (target & (cells - 1))
    spread = jnp.where(iota((width, 8 * cells), 0) == target, 1.0, 0.0).astype(BF16)
    diagonal = (iota((1, 8 * cells), 1) // cells) == iota((8, 1), 0)
    slot_line = iota((slots, 1), 0)

    inputs[0].wait()
    inputs[1].wait()
    owner = owner_v[...]
    live = iota((1, blocks), 1) < busy_ref[0]
    label = jnp.where(live, owner * owned + place_v[...], -1)
    lab_all[chip] = label

    ownerf = owner.astype(F32)
    earlier = (
        (to_column(ownerf) == ownerf)
        & (iota((blocks, blocks), 0) < iota((blocks, blocks), 1))
        & (iota((blocks, blocks), 0) < busy_ref[0])
    )
    rank = jnp.sum(jnp.where(earlier, 1.0, 0.0), axis=0, keepdims=True).astype(I32)
    slot = jnp.where((owner & 1) == core, 0, sources) + (owner >> 1) * 2 + rank
    slot = jnp.where(live, slot, -1)
    slot_column = to_column(slot.astype(F32))
    to_slots = jnp.where(slot_line == slot, 1.0, 0.0).astype(BF16)
    from_slots = jnp.where(
        iota((1, slots), 1).astype(F32) == slot_column, 1.0, 0.0
    ).astype(BF16)

    pl.semaphore_wait(barrier, chips - 1 + nrep - 1 + 1)

    for other, device in others:
        send(0, lab_all.at[chip], lab_all.at[chip], device)
    inputs[2].wait()
    fields = send(1, field_v, field_x, sibling)

    second = (iota((sources, blocks), 0) & 1) == 1
    key_lane = iota((sources, blocks), 1) * owned

    def spread_out(table):
        return jnp.broadcast_to(table[...], (chips, 2, blocks)).reshape(sources, blocks)

    def find(labels, owner_id):
        place = labels - owner_id * owned
        match = (place >= 0) & (place < owned)
        key = (key_lane + place).astype(F32)
        key = jnp.where(match, jnp.where(second, -key, key), ABSENT)
        key = jnp.abs(jnp.min(key, axis=1, keepdims=True))
        return key - jnp.floor(key * (1.0 / owned)) * owned

    arrived(0, lab_all.at[pl.ds(0, chips - 1)])
    labels = send(2, lab_all, lab_x, sibling)

    table = spread_out(lab_all)
    field_lane = iota((1, owned), 1).astype(F32)

    def serve(i, wanted, field):
        picks = jnp.where(field_lane == wanted, 1.0, 0.0).astype(BF16)
        row_s[i] = dot(picks, field[...]).astype(BF16).reshape(chips, 2, width)

    far, near = others[: len(others) // 4], others[len(others) // 4 :]
    here = find(table, me)
    serve(0, here, field_v)
    for other, device in far:
        send(3, row_s.at[0, other], row_r.at[0, chip], device)
    place = find(table, chip * 2 + (1 - core))
    fields.wait()
    serve(1, place, field_x)
    for other, device in far:
        send(3, row_s.at[1, other], row_r.at[1, chip], device)
    for other, device in near:
        send(3, row_s.at[:, other], row_r.at[:, chip], device)
    row_r[:, chip] = row_s[:, chip]

    labels.wait()
    for i, place in enumerate((here, find(spread_out(lab_x), me))):
        lines = jnp.where(iota((owned, 1), 0).astype(F32) == to_row(place), 1.0, 0.0)
        deposits[:, :, i * sources : (i + 1) * sources] = lines.astype(BF16).reshape(
            nrep, owned // nrep, sources
        )
    arrived(3, row_r.at[:, pl.ds(0, chips - 1)])

    gas = dot(from_slots, row_r[...].reshape(slots, width))
    gas = dot(gas.astype(BF16), spread)
    for copy in inputs[3:]:
        copy.wait()
    pair = 2 * cells
    sampled = []
    for g in range(blocks // 8):
        left = []
        for c in range(4):
            piece = gas[8 * g : 8 * g + 8, c * pair : (c + 1) * pair]
            left.append(
                jnp.where(diagonal, jnp.concatenate([piece] * 4, axis=1), 0.0)
            )
        left = jnp.concatenate(left, axis=0).astype(BF16)
        sampled.append(
            dot(left, tiles[8 * g : 8 * g + 8].reshape(8 * cells, parcels))
        )
    scale = 2.0 / cells
    u = [
        jnp.concatenate([s[8 * c : 8 * c + 8] for s in sampled], axis=0) * scale
        for c in range(4)
    ]

    v = [speed[c] for c in range(3)]
    d = size[...]
    t = heat[...]
    slip = [u[c] - v[c] for c in range(3)]
    slip_speed = jnp.sqrt(
        1.0 + (slip[0] * slip[0] + slip[1] * slip[1] + slip[2] * slip[2])
    )
    reynolds = REYNOLDS_SCALE * d * slip_speed
    squared = d * d
    drag = DRAG_SCALE * (1.0 + 0.15 * jnp.exp(0.687 * jnp.log(reynolds))) / squared
    warm = HEAT_SCALE * (2.0 + 0.6 * PRANDTL_ROOT * jnp.sqrt(reynolds)) / squared
    mass = LOADING * d * squared
    live_column = slot_column >= 0.0
    terms = []
    for c in range(3):
        new = (v[c] + drag * u[c]) / (1.0 + drag)
        terms.append((-mass * (new - v[c])).astype(BF16))
        moved[c] = jnp.where(live_column, new, v[c])
    new = (t + warm * u[3]) / (1.0 + warm)
    terms.append((-mass * (new - t)).astype(BF16))
    warmed[...] = jnp.where(live_column, new, t)
    outputs = [
        pltpu.make_async_copy(src, dst, out_sem.at[i])
        for i, (src, dst) in enumerate(((moved, moved_hbm), (warmed, warmed_hbm)))
    ]
    for copy in outputs:
        copy.start()

    lane, line = iota((32, pair), 1), iota((32, pair), 0)
    line = line & 7
    low = iota((8, pair), 1) < cells
    rows = []
    termf = [x.astype(F32) for x in terms]
    for g in range(blocks // 8):
        left = jnp.concatenate([x[8 * g : 8 * g + 8] for x in termf], axis=0)
        full = lax.dot_general(
            left.astype(BF16),
            tiles[8 * g : 8 * g + 8].reshape(8 * cells, parcels),
            (((1,), (1,)), ((), ())),
            preferred_element_type=F32,
        )
        own = jnp.zeros((32, pair), F32)
        for j in range(4):
            keep = line == 2 * j + lane // cells
            own = own + jnp.where(keep, full[:, j * pair : (j + 1) * pair], 0.0)
        own = own + pltpu.roll(own, cells, axis=1)
        rows.append(
            jnp.concatenate(
                [
                    jnp.where(low, own[0:8], own[8:16]),
                    jnp.where(low, own[16:24], own[24:32]),
                ],
                axis=1,
            )
        )
    code = encode(jnp.concatenate(rows, axis=0) * scale)
    high = jnp.floor(code * (1.0 / 256.0)) * 256.0
    code = [high.astype(BF16), (code - high).astype(BF16)]

    def in_slots(lines):
        code_there = dot(lines, code[0]) + dot(lines, code[1])
        return code_there.astype(I32).astype(I16).reshape(chips, 2, width)

    sums_x[...] = in_slots(to_slots[sources:])
    copy = send(5, sums_x, sums_s.at[1], sibling)
    sums_s[0] = in_slots(to_slots[:sources])
    far, near = others[: len(others) // 2], others[len(others) // 2 :]
    for other, device in far:
        send(6, sums_s.at[0, other], sums_r.at[0, chip], device)
    copy.wait()
    for other, device in far:
        send(6, sums_s.at[1, other], sums_r.at[1, chip], device)
    for other, device in near:
        send(6, sums_s.at[:, other], sums_r.at[:, chip], device)
    sums_r[:, chip] = sums_s[:, chip]

    arrived(6, sums_r.at[:, pl.ds(0, chips - 1)])
    high, rest = halves(decode(sums_r[...].reshape(slots, width)))
    for step, other, device in reps:
        lines = deposits[other]
        total = dot(lines, high) + dot(lines, rest)
        if step:
            part_s[step - 1] = encode(total, PART_CODES).astype(I32).astype(I16)
            send(8, part_s.at[step - 1], part_r.at[step - 1], device)
    arrived(8, part_r)
    for k in range(nrep - 1):
        total = total + decode(part_r[k], PART_CODES)
    source_ref[...] = total
    for copy in outputs:
        copy.wait()


def hand_over(count, *refs):
    sources, results, held = (refs[i * count : (i + 1) * count] for i in range(3))
    sem_in, sem_out = refs[3 * count :]
    arrive = [
        pltpu.make_async_copy(sources[i], held[i], sem_in.at[i]) for i in range(count)
    ]
    leave = [
        pltpu.make_async_copy(held[i], results[i], sem_out.at[i]) for i in range(count)
    ]
    for copy in arrive:
        copy.start()
    for i in range(count):
        arrive[i].wait()
        leave[i].start()
    for copy in leave:
        copy.wait()


def per_device(
    ny,
    nz,
    nrep,
    particle_speeds,
    particle_diameters,
    particle_kelvins,
    unscaled_kernel_coefficients,
    bundle_patch_ordinal,
    bundle_patch_custodian,
    busy_bundles_per_accelerator,
    ambient_flow_quantities,
):
    blocks, cells, parcels = unscaled_kernel_coefficients.shape
    owned, width = ambient_flow_quantities.shape
    chips = ny * nz
    hbm = pl.BlockSpec(memory_space=pltpu.HBM)
    vmem = pl.BlockSpec(memory_space=pltpu.VMEM)
    smem = pl.BlockSpec(memory_space=pltpu.SMEM)
    results = pl.pallas_call(
        functools.partial(step_kernel, ny, nz, nrep),
        out_shape=(
            jax.ShapeDtypeStruct((3, blocks, parcels), F32),
            jax.ShapeDtypeStruct((blocks, parcels), F32),
            jax.ShapeDtypeStruct((owned // nrep, width), F32),
        ),
        in_specs=[hbm, hbm, smem] + [hbm] * 5,
        out_specs=(hbm, hbm, vmem),
        scratch_shapes=[
            pltpu.VMEM((1, blocks), I32),
            pltpu.VMEM((1, blocks), I32),
            pltpu.VMEM((owned, width), BF16),
            pltpu.VMEM((blocks, cells, parcels), BF16),
            pltpu.VMEM((3, blocks, parcels), F32),
            pltpu.VMEM((blocks, parcels), F32),
            pltpu.VMEM((blocks, parcels), F32),
            pltpu.VMEM((3, blocks, parcels), F32),
            pltpu.VMEM((blocks, parcels), F32),
            pltpu.VMEM((owned, width), BF16),
            pltpu.VMEM((chips, 1, blocks), I32),
            pltpu.VMEM((chips, 1, blocks), I32),
            pltpu.VMEM((2, chips, 2, width), BF16),
            pltpu.VMEM((2, chips, 2, width), BF16),
            pltpu.VMEM((chips, 2, width), I16),
            pltpu.VMEM((2, chips, 2, width), I16),
            pltpu.VMEM((2, chips, 2, width), I16),
            pltpu.VMEM((nrep, owned // nrep, 4 * chips), BF16),
            pltpu.VMEM((nrep - 1, owned // nrep, width), I16),
            pltpu.VMEM((nrep - 1, owned // nrep, width), I16),
            pltpu.SemaphoreType.DMA((7,)),
            pltpu.SemaphoreType.DMA((2,)),
            pltpu.SemaphoreType.DMA((9,)),
            pltpu.SemaphoreType.DMA((9,)),
        ],
        compiler_params=pltpu.CompilerParams(
            collective_id=0, has_side_effects=True, vmem_limit_bytes=63 * 2**20
        ),
        name="parcel_step",
    )(
        bundle_patch_custodian.reshape(1, blocks),
        bundle_patch_ordinal.reshape(1, blocks),
        busy_bundles_per_accelerator,
        ambient_flow_quantities,
        unscaled_kernel_coefficients,
        jnp.transpose(particle_speeds, (1, 0, 2)),
        particle_diameters,
        particle_kelvins,
    )
    moved, warmed, source = pl.pallas_call(
        functools.partial(hand_over, 3),
        out_shape=tuple(jax.ShapeDtypeStruct(x.shape, x.dtype) for x in results),
        in_specs=[hbm] * 3,
        out_specs=(hbm, hbm, hbm),
        scratch_shapes=[pltpu.VMEM(x.shape, x.dtype) for x in results]
        + [pltpu.SemaphoreType.DMA((3,))] * 2,
        compiler_params=pltpu.CompilerParams(vmem_limit_bytes=63 * 2**20),
        name="hand_over",
    )(*results)
    return jnp.transpose(moved, (1, 0, 2)), warmed, source


def solution(mesh, ny=4, nz=16):
    both = ("cells", "rep")
    return jax.shard_map(
        functools.partial(per_device, ny, nz, mesh.shape["rep"]),
        mesh=mesh,
        in_specs=(
            P(both, None, None),
            P(both, None),
            P(both, None),
            P(both, None, None),
            P(both),
            P(both),
            P(both),
            P("cells", None),
        ),
        out_specs=(P(both, None, None), P(both, None), P(both, None)),
        check_vma=False,
    )
```
